256 devices in a mesh: seq: 64 (over z_hi, y, x, core), tp: 4 (over z_lo).
Axes of the slice: x: 4, y: 4, z: 8 (z_hi: 2, z_lo: 4; z = z_hi * 4 + z_lo), core: 2. Of those that a mesh axis runs over, the one named last changes fastest.
Arguments:
- tokens: bfloat16 [8192, 4096], P('seq', 'tp'), may hold values from -6 to 6
- in_weight: bfloat16 [3, 4096, 2048], P(None, 'seq', 'tp'), may hold values from -0.09375 to 0.09375
- short_weight: float32 [3, 3, 2048], P(None, None, 'tp'), may hold values from -3 to 3
- residues: float32 [2048, 8], P('tp'), may hold values from -0.6 to 0.6
- decay_rates: float32 [2048, 8], P('tp'), may hold values from 0.00012207031 to 0.0625
- skip_gain: float32 [2048], P('tp'), may hold values from -2 to 2
- out_weight: bfloat16 [2048, 4096], P('tp', 'seq'), may hold values from -0.125 to 0.125
Outputs:
- layer_out: bfloat16 [8192, 4096], P('seq', 'tp')
The draws below stay inside these ranges and needn't reach their ends.
All inputs are finite; a program needn't handle non-finite values.
Results may differ from the reference program's by a relative error of at most 0.005.
The reference program's roundings to bfloat16 on the way (of `projected` and `gate_out`) count: a program that leaves them out, or rounds other values in their place, can miss the bound.
Values may be sent and summed in bfloat16 or wider, within the bound.
No kernel may reach another device: no remote copies, remote signals or barrier semaphores. Data moves between devices by JAX's collectives and lax.ppermute only.
A program may use at most 64 MiB of HBM per device.

```python
import math
import jax
import jax.numpy as jnp
from jax import lax

D = 4096
C = 2048
SHORT = 3
MODES = 8
TOKENS = 8192


def levels(rng, shape, split, least, largest):
    loudness, own = 1.0, jax.random.fold_in(rng, 6)
    for dim, parts in split:
        steps = jnp.exp(jax.random.uniform(jax.random.fold_in(own, dim), (parts,), jnp.float32, least / len(split), largest / len(split)))
        loudness = loudness * jnp.repeat(steps, shape[dim] // parts).reshape([-1 if axis == dim else 1 for axis in range(len(shape))])
    return loudness


def noise(stream_key, extent, scale, limit, split=(), dtype=jnp.bfloat16):
    gain = levels(stream_key, extent, split, -0.22, 0.18) if split else 1.0
    result = jax.random.normal(stream_key, extent, jnp.float32) * scale * gain
    return jnp.minimum(jnp.maximum(result, -limit), limit).astype(dtype)


def setup_inputs(seed: int = 0) -> dict:
    key_list = jax.random.split(jax.random.key(seed), 8)
    return {
        "tokens": noise(key_list[0], (TOKENS, D), 1.0, 6.0, ((0, 64), (1, 4))),
        "in_weight": noise(key_list[1], (3, D, C), D ** -0.5, 0.09375, ((1, 64), (2, 4))),
        "short_weight": noise(key_list[2], (3, SHORT, C), 0.6, 3.0, ((2, 4),), jnp.float32),
        "residues": noise(key_list[3], (C, MODES), 0.1, 0.6, ((0, 4),), jnp.float32),
        "decay_rates": jnp.clip(jnp.exp(math.log(0.0625) - 6.2383246 * jax.random.uniform(key_list[4], (C, MODES), jnp.float32) ** levels(key_list[4], (C, MODES), ((0, 4),), -0.2, 0.2)), 0.00012207031, 0.0625),
        "skip_gain": noise(key_list[5], (C,), 0.5, 2.0, ((0, 4),), jnp.float32),
        "out_weight": noise(key_list[6], (C, D), C ** -0.5, 0.125, ((0, 4), (1, 64))),
    }


def reference(tokens, in_weight, short_weight, residues, decay_rates, skip_gain, out_weight):
    projected = jnp.stack([jnp.dot(tokens, in_weight[stream], preferred_element_type=jnp.float32) for stream in range(3)])
    projected = lax.optimization_barrier(projected.astype(jnp.bfloat16)).astype(jnp.float32)
    padded = jnp.pad(projected, ((0, 0), (SHORT - 1, 0), (0, 0)))
    streams = jnp.zeros_like(projected)
    for tap_index in range(SHORT):
        lead_rows = SHORT - 1 - tap_index
        streams = streams + short_weight[:, tap_index, None, :] * padded[:, lead_rows:lead_rows + TOKENS, :]
    gated_input = streams[0] * streams[2]
    positions = jnp.arange(TOKENS).astype(jnp.float32)
    response = jnp.zeros((TOKENS, C), jnp.float32)
    for mode_index in range(MODES):
        response = response + residues[:, mode_index] * jnp.exp(-decay_rates[:, mode_index] * positions[:, None])
    fft_length = 2 * TOKENS
    spectrum = jnp.fft.rfft(gated_input, n=fft_length, axis=0) * jnp.fft.rfft(response, n=fft_length, axis=0)
    convolved = jnp.fft.irfft(spectrum, n=fft_length, axis=0)[:TOKENS]
    mixed = convolved + skip_gain * gated_input
    gate_out = (streams[1] * mixed).astype(jnp.bfloat16)
    return jnp.dot(gate_out, out_weight, preferred_element_type=jnp.float32).astype(jnp.bfloat16)
```

```python
import functools

import jax
import jax.numpy as jnp
import numpy as np
from jax import lax
from jax.experimental import pallas as pl
from jax.experimental.pallas import tpu as pltpu
from jax.sharding import Mesh, PartitionSpec as P

AXES = ("zh", "y", "x", "c", "zl")
SIZES = (2, 4, 4, 2, 4)
SEQ = ("zh", "y", "x", "c")
CHIPS = 16
BLOCK = 256
HALF = 128
LANES = 128
WIDE = 3 * LANES
MODES = 8
SUB = 8
STEPS = BLOCK // SUB
HALO = 16
GROUP = 64
F32 = jnp.float32
BF16 = jnp.bfloat16


def shifted(block, axis, distance):
    count = lax.axis_size(axis)
    return lax.ppermute(block, axis, [(i, (i + distance) % count) for i in range(count)])


def ring(block, axis):
    half = block.shape[0] // 2
    low = shifted(block, axis, 1)
    high = shifted(block, axis, -1)
    far_low = shifted(low[:half], axis, 1)
    far_high = shifted(high[half:], axis, -1)
    return [block, low, high, far_low, far_high]


RING_OFFSETS = ((0, None), (-1, None), (1, None), (2, 0), (2, 1))


def ring_pieces(pieces):
    half = len(pieces) // 2
    arrays = []
    for offset, part in RING_OFFSETS:
        kept = pieces if part is None else pieces[part * half : (part + 1) * half]
        arrays.append([(offset, piece) for piece in kept])
    return arrays


def front_kernel(
    pos,
    slabs,
    a0, a1, a2, a3, a4,
    b0, b1, b2, b3, b4,
    taps,
    rates,
    residues,
    skip,
    y_out,
    gate_out,
    sub_out,
    total_out,
    lhs,
    rhs,
    proj,
    gated,
    weight_sem,
    token_sem,
):
    own_y, own_x, own_zh, own_c = pos[0], pos[1], pos[2], pos[3]
    copies = []
    count = 0
    for kz, arrays in ((0, (a0, a1, a2, a3, a4)), (1, (b0, b1, b2, b3, b4))):
        first = [piece for array in ring_pieces([0, 1]) for piece in array]
        for ref, pieces in zip(arrays, ring_pieces(first)):
            for place, (outer, (inner, kc)) in enumerate(pieces):
                dy, dx = (outer, inner) if kz == 0 else (inner, outer)
                at_y = lax.rem(own_y + (dy + 4), 4)
                at_x = lax.rem(own_x + (dx + 4), 4)
                at_zh = own_zh if kz == 0 else 1 - own_zh
                at_c = own_c if kc == 0 else 1 - own_c
                row = (((at_zh * 4 + at_y) * 4 + at_x) * 2 + at_c) * GROUP
                copies.append(
                    pltpu.make_async_copy(
                        ref.at[pl.ds(place * GROUP, GROUP)],
                        rhs.at[pl.ds(pl.multiple_of(row, GROUP), GROUP)],
                        weight_sem.at[count],
                    )
                )
                count += 1
    for zh in range(2):
        for zl in range(4):
            for c in range(2):
                skipped = HALO * c
                rows = HALO + HALF - skipped
                copies.append(
                    pltpu.make_async_copy(
                        slabs.at[(zh * 4 + zl) * 2 + c, pl.ds(skipped, rows)],
                        lhs.at[
                            pl.ds(zh * (HALO + BLOCK) + c * (HALO + HALF), rows),
                            pl.ds(zl * 1024, 1024),
                        ],
                        token_sem.at[(zh * 4 + zl) * 2 + c],
                    )
                )
    for copy in copies:
        copy.start()
    for copy in copies:
        copy.wait()
    proj[...] = (
        jnp.dot(lhs[...], rhs[...], preferred_element_type=F32).astype(BF16).astype(F32)
    )
    gain = skip[...]
    for zh in range(2):
        base = zh * (HALO + BLOCK) + HALO
        streams = []
        for s in range(3):
            total = jnp.zeros((BLOCK, LANES), F32)
            for m in range(3):
                tap = taps[3 * s + m : 3 * s + m + 1, :]
                total = total + tap * proj[base - m : base - m + BLOCK, s * LANES : (s + 1) * LANES]
            streams.append(total)
        gated[zh * BLOCK : (zh + 1) * BLOCK, :] = streams[0] * streams[2]
        gate_out[zh * BLOCK : (zh + 1) * BLOCK, :] = streams[1]
    rate = rates[...]
    decay = jnp.exp(-rate)
    weight = residues[...]
    decays = [jnp.broadcast_to(decay[m : m + 1], (SUB, LANES)) for m in range(MODES)]
    weights = [jnp.broadcast_to(weight[m : m + 1], (SUB, LANES)) for m in range(MODES)]
    gain = jnp.broadcast_to(gain, (SUB, LANES))
    long_decay = jnp.exp(-rate * float(STEPS))
    for zh in range(2):
        state = [jnp.zeros((SUB, LANES), F32) for _ in range(MODES)]
        for i in range(STEPS):
            rows = pl.ds(zh * BLOCK + i, SUB, stride=STEPS)
            entry = gated[rows, :]
            state = [decays[m] * state[m] + entry for m in range(MODES)]
            terms = [weights[m] * state[m] for m in range(MODES)]
            while len(terms) > 1:
                terms = [terms[k] + terms[k + 1] for k in range(0, len(terms), 2)]
            y_out[rows, :] = terms[0] + gain * entry
        for m in range(MODES):
            sub_out[pl.ds(zh * SUB * MODES + m, SUB, stride=MODES), :] = state[m]
        total = jnp.zeros((MODES, LANES), F32)
        for sub in range(SUB):
            start = zh * SUB * MODES + sub * MODES
            total = long_decay * total + sub_out[start : start + MODES, :]
        total_out[zh * MODES : (zh + 1) * MODES, :] = total


def front(pos, slabs, a, b, taps, rates, residues, skip):
    hbm = pl.BlockSpec(memory_space=pl.ANY)
    vmem = pl.BlockSpec(memory_space=pltpu.VMEM)
    smem = pl.BlockSpec(memory_space=pltpu.SMEM)
    rows = 2 * (HALO + BLOCK)
    return pl.pallas_call(
        front_kernel,
        out_shape=(
            jax.ShapeDtypeStruct((2 * BLOCK, LANES), F32),
            jax.ShapeDtypeStruct((2 * BLOCK, LANES), F32),
            jax.ShapeDtypeStruct((2 * SUB * MODES, LANES), F32),
            jax.ShapeDtypeStruct((2 * MODES, LANES), F32),
        ),
        in_specs=[smem] + [hbm] * 11 + [vmem] * 4,
        out_specs=(vmem,) * 4,
        scratch_shapes=[
            pltpu.VMEM((rows, 4096), BF16),
            pltpu.VMEM((4096, WIDE), BF16),
            pltpu.VMEM((rows, WIDE), F32),
            pltpu.VMEM((2 * BLOCK, LANES), F32),
            pltpu.SemaphoreType.DMA((64,)),
            pltpu.SemaphoreType.DMA((16,)),
        ],
        compiler_params=pltpu.CompilerParams(vmem_limit_bytes=40 * 1024 * 1024),
        cost_estimate=pl.CostEstimate(
            flops=2 * rows * 4096 * WIDE, bytes_accessed=6_000_000, transcendentals=0
        ),
    )(pos, slabs, *a, *b, taps, rates, residues, skip)


def back_kernel(pos, totals, sub_states, y_in, gate_in, rates, residues, out, carried, mixed):
    block = pos[0] * 4 + pos[1]
    rate = rates[...]
    weight = residues[...]
    decay = jnp.exp(-rate)
    long_decay = jnp.exp(-rate * float(STEPS))
    carry = [jnp.zeros((MODES, LANES), F32) for _ in range(2)]
    for other in range(CHIPS):
        distance = block - 1 - other
        span = jnp.maximum(distance, 0).astype(F32) * float(BLOCK)
        near = jnp.where(distance >= 0, jnp.exp(-rate * span), 0.0)
        far = jnp.exp(-rate * ((distance + CHIPS).astype(F32) * float(BLOCK)))
        first = totals[2 * MODES * other : 2 * MODES * other + MODES, :]
        second = totals[2 * MODES * other + MODES : 2 * MODES * (other + 1), :]
        carry[0] = carry[0] + near * first
        carry[1] = carry[1] + near * second + far * first
    decays = [jnp.broadcast_to(decay[m : m + 1], (SUB, LANES)) for m in range(MODES)]
    for zh in range(2):
        state = carry[zh]
        for sub in range(SUB):
            start = zh * SUB * MODES + sub * MODES
            carried[start : start + MODES, :] = weight * state
            state = long_decay * state + sub_states[start : start + MODES, :]
        terms = [
            carried[pl.ds(zh * SUB * MODES + m, SUB, stride=MODES), :] for m in range(MODES)
        ]
        for i in range(STEPS):
            rows = pl.ds(zh * BLOCK + i, SUB, stride=STEPS)
            terms = [decays[m] * terms[m] for m in range(MODES)]
            sums = terms
            while len(sums) > 1:
                sums = [sums[k] + sums[k + 1] for k in range(0, len(sums), 2)]
            mixed[rows, :] = gate_in[rows, :] * (y_in[rows, :] + sums[0])
    out[...] = mixed[...].astype(BF16)


def back(pos, totals, sub_states, y, gate, rates, residues):
    vmem = pl.BlockSpec(memory_space=pltpu.VMEM)
    smem = pl.BlockSpec(memory_space=pltpu.SMEM)
    return pl.pallas_call(
        back_kernel,
        out_shape=jax.ShapeDtypeStruct((2 * BLOCK, LANES), BF16),
        in_specs=[smem] + [vmem] * 6,
        out_specs=vmem,
        scratch_shapes=[
            pltpu.VMEM((2 * SUB * MODES, LANES), F32),
            pltpu.VMEM((2 * BLOCK, LANES), F32),
        ],
        compiler_params=pltpu.CompilerParams(vmem_limit_bytes=16 * 1024 * 1024),
        cost_estimate=pl.CostEstimate(
            flops=4_000_000, bytes_accessed=800_000, transcendentals=40_000
        ),
    )(pos, totals, sub_states, y, gate, rates, residues)


def out_kernel(pos, gates, weights, out, held, sem):
    own_zh = pos[2]
    copies = []
    for k in range(2):
        for half in range(2):
            place = (own_zh if k == 0 else 1 - own_zh) * 2 + half
            copies.append(
                pltpu.make_async_copy(
                    weights.at[pl.ds(16 * half, 16), k], held.at[place], sem.at[2 * k + half]
                )
            )
    for copy in copies:
        copy.start()
    for copy in copies:
        copy.wait()
    total = jnp.zeros((HALF, 1024), F32)
    for zl in range(4):
        parts = [gates[(2 * zh + c) * 4 + zl] for zh in range(2) for c in range(2)]
        total = total + lax.dot_general(
            jnp.concatenate(parts, axis=1),
            held[zl].reshape(1024, 512),
            (((1,), (1,)), ((), ())),
            preferred_element_type=F32,
        )
    out[...] = total.astype(BF16)


def project_out(pos, gates, weights):
    hbm = pl.BlockSpec(memory_space=pl.ANY)
    vmem = pl.BlockSpec(memory_space=pltpu.VMEM)
    smem = pl.BlockSpec(memory_space=pltpu.SMEM)
    return pl.pallas_call(
        out_kernel,
        out_shape=jax.ShapeDtypeStruct((HALF, 1024), BF16),
        in_specs=[smem, vmem, hbm],
        out_specs=vmem,
        scratch_shapes=[
            pltpu.VMEM((4, 16, 64, 512), BF16),
            pltpu.SemaphoreType.DMA((4,)),
        ],
        compiler_params=pltpu.CompilerParams(vmem_limit_bytes=32 * 1024 * 1024),
        cost_estimate=pl.CostEstimate(
            flops=2 * HALF * 2048 * 1024, bytes_accessed=5_000_000, transcendentals=0
        ),
    )(pos, gates, weights)


def transposed_routes():
    near, far = [], []
    for zh, y, x, c, zl in np.ndindex(*SIZES):
        source = int(np.ravel_multi_index((zh, y, x, c, zl), SIZES))
        for route, to_zh in ((near, zl // 2), (far, 1 - zl // 2)):
            target = (to_zh, (zl % 2) * 2 + y % 2, x, c, zh * 2 + y // 2)
            route.append((source, int(np.ravel_multi_index(target, SIZES))))
    return near, far


def shards(tokens, in_weight, short_weight, residues, decay_rates, skip_gain, out_weight):
    zh, y, x, c = (lax.axis_index(axis) for axis in SEQ)
    pos = jnp.stack([y, x, zh, c]).astype(jnp.int32)
    group = zh * 2 + c

    halo = lax.ppermute(tokens[HALF - HALO :], SEQ, [(i, i + 1) for i in range(63)])
    slab = jnp.concatenate([halo, tokens], axis=0)
    slabs = lax.all_gather(slab, ("zh", "zl", "c"), axis=0, tiled=False)

    quarters = in_weight.reshape(3, GROUP, 4, LANES).transpose(2, 1, 0, 3).reshape(4, GROUP, WIDE)

    def quarter(flip):
        part = lax.dynamic_index_in_dim(quarters, group ^ flip, 0, keepdims=False)
        if flip == 0:
            return part
        return lax.ppermute(part, ("zh", "c"), [(i, i ^ flip) for i in range(4)])

    near = jnp.concatenate([quarter(0), quarter(1)], axis=0)
    far = jnp.concatenate([quarter(2), quarter(3)], axis=0)
    a = ring(jnp.concatenate(ring(near, "x"), axis=0), "y")
    b = ring(jnp.concatenate(ring(far, "y"), axis=0), "x")

    columns = out_weight.T
    routes = transposed_routes()
    gathered = lax.all_gather(
        jnp.stack([lax.ppermute(columns, AXES, route) for route in routes]),
        ("y", "x", "c"),
        axis=0,
        tiled=False,
    )

    def own_channels(table, axis):
        return lax.dynamic_slice_in_dim(table, group * LANES, LANES, axis)

    taps = own_channels(short_weight, 2).reshape(9, LANES)
    rates = own_channels(decay_rates, 0).T
    weights = own_channels(residues, 0).T
    skip = own_channels(skip_gain, 0)[None]
    mixed, gate, sub_states, totals = front(pos, slabs, a, b, taps, rates, weights, skip)
    every = lax.all_to_all(
        jnp.broadcast_to(totals[None], (CHIPS,) + totals.shape),
        ("y", "x"),
        split_axis=0,
        concat_axis=0,
        tiled=True,
    ).reshape(CHIPS * 2 * MODES, LANES)
    gate_out = back(pos, every, sub_states, mixed, gate, rates, weights)
    sent = jnp.broadcast_to(gate_out.reshape(4, 1, HALF, LANES), (4, 4, HALF, LANES))
    gates = lax.all_to_all(
        sent.reshape(16, HALF, LANES), ("zh", "c", "zl"), split_axis=0, concat_axis=0, tiled=True
    )
    return project_out(pos, gates, gathered)


def solution(mesh):
    split_mesh = Mesh(mesh.devices.reshape(SIZES), AXES)
    return jax.shard_map(
        shards,
        mesh=split_mesh,
        in_specs=(
            P(SEQ, "zl"),
            P(None, SEQ, "zl"),
            P(None, None, "zl"),
            P("zl", None),
            P("zl", None),
            P("zl"),
            P("zl", SEQ),
        ),
        out_specs=P(SEQ, "zl"),
        check_vma=False,
    )
```

```python
import functools

import jax
import jax.numpy as jnp
import numpy as np
from jax import lax
from jax.experimental import pallas as pl
from jax.experimental.pallas import tpu as pltpu
from jax.sharding import Mesh, PartitionSpec as P

AXES = ("zh", "y", "x", "c", "zl")
SIZES = (2, 4, 4, 2, 4)
SEQ = ("zh", "y", "x", "c")
CHIPS = 16
BLOCK = 256
HALF = 128
LANES = 128
WIDE = 3 * LANES
MODES = 8
SUB = 8
STEPS = BLOCK // SUB
EDGE = 2 * MODES
EDGE_ROWS = 40
GROUP = 64
F32 = jnp.float32
BF16 = jnp.bfloat16


def crossed(block, phase, distance):
    route = []
    for y, x, c in np.ndindex(4, 4, 2):
        target = (y, (x + distance) % 4, c) if c == phase else ((y + distance) % 4, x, c)
        route.append((int(np.ravel_multi_index((y, x, c), (4, 4, 2))), int(np.ravel_multi_index(target, (4, 4, 2)))))
    return lax.ppermute(block, ("y", "x", "c"), route)


def ring(block, phase):
    half = block.shape[0] // 2
    low = crossed(block, phase, 1)
    high = crossed(block, phase, -1)
    far_low = crossed(low[:half], phase, 1)
    far_high = crossed(high[half:], phase, -1)
    return [block, low, high, far_low, far_high]


RING_ORDER = (0, -1, 1, 2)


def front_kernel(
    pos,
    slabs,
    w0, w1, w2, w3, w4,
    taps,
    rates,
    residues,
    skip,
    y_out,
    gate_out,
    sub_out,
    edge_out,
    proj,
    gated,
):
    own_y, own_x, own_zh, own_c = pos[0], pos[1], pos[2], pos[3]

    def features(outer, inner, half):
        first = RING_ORDER[outer] + 4
        second = RING_ORDER[inner] + 4
        at_y = lax.rem(own_y + jnp.where(own_c == 0, first, second), 4)
        at_x = lax.rem(own_x + jnp.where(own_c == 0, second, first), 4)
        at_zh = own_zh if half == 0 else 1 - own_zh
        zl = at_zh * 2 + at_y // 2
        lane = pl.multiple_of((lax.rem(at_y, 2) * 4 + at_x) * 128, 128)
        return slabs[:, pl.ds(zl, 1), :, :, pl.ds(lane, 128)].reshape(2 * BLOCK, 128)

    total = None
    place = 0
    for array in (w0, w1, w2, w3, w4):
        count = array.shape[0] // 256
        parts = [
            features((place + k) // 4, (place + k) % 4, half)
            for k in range(count)
            for half in range(2)
        ]
        part = jnp.dot(jnp.concatenate(parts, axis=1), array[...], preferred_element_type=F32)
        total = part if total is None else total + part
        place += count
    proj[:, 0:8, :] = jnp.zeros((2, 8, WIDE), F32)
    proj[:, 8:, :] = total.astype(BF16).astype(F32).reshape(2, BLOCK, WIDE)
    gain = skip[...]
    for zh in range(2):
        streams = []
        edges = []
        for s in range(3):
            lanes = slice(s * LANES, (s + 1) * LANES)
            tap = [taps[3 * s + m : 3 * s + m + 1, :] for m in range(3)]
            total = jnp.zeros((BLOCK, LANES), F32)
            for m in range(3):
                total = total + tap[m] * proj[zh, 8 - m : 8 - m + BLOCK, lanes]
            streams.append(total)
            before = proj[zh, BLOCK + 6 : BLOCK + 7, lanes]
            last = proj[zh, BLOCK + 7 : BLOCK + 8, lanes]
            edges.append([tap[1] * last + tap[2] * before, tap[2] * last])
        gated[zh * BLOCK : (zh + 1) * BLOCK, :] = streams[0] * streams[2]
        gate_out[zh * BLOCK : (zh + 1) * BLOCK, :] = streams[1]
        rows = [streams[0][0:1], streams[0][1:2], streams[2][0:1], streams[2][1:2]]
        rows = rows + edges[0] + edges[2] + edges[1]
        for chip in range(CHIPS):
            for k, row in enumerate(rows):
                edge_out[chip, EDGE + zh * 10 + k : EDGE + zh * 10 + k + 1, :] = row
    rate = rates[...]
    decay = jnp.exp(-rate)
    weight = residues[...]
    decays = [jnp.broadcast_to(decay[m : m + 1], (SUB, LANES)) for m in range(MODES)]
    weights = [jnp.broadcast_to(weight[m : m + 1], (SUB, LANES)) for m in range(MODES)]
    gain = jnp.broadcast_to(gain, (SUB, LANES))
    long_decay = jnp.exp(-rate * float(STEPS))
    for zh in range(2):
        state = [jnp.zeros((SUB, LANES), F32) for _ in range(MODES)]
        for i in range(STEPS):
            rows = pl.ds(zh * BLOCK + i, SUB, stride=STEPS)
            entry = gated[rows, :]
            state = [decays[m] * state[m] + entry for m in range(MODES)]
            terms = [weights[m] * state[m] for m in range(MODES)]
            while len(terms) > 1:
                terms = [terms[k] + terms[k + 1] for k in range(0, len(terms), 2)]
            y_out[rows, :] = terms[0] + gain * entry
        for m in range(MODES):
            sub_out[pl.ds(zh * SUB * MODES + m, SUB, stride=MODES), :] = state[m]
        total = jnp.zeros((MODES, LANES), F32)
        for sub in range(SUB):
            start = zh * SUB * MODES + sub * MODES
            total = long_decay * total + sub_out[start : start + MODES, :]
        for chip in range(CHIPS):
            edge_out[chip, zh * MODES : (zh + 1) * MODES, :] = total


def front(pos, slabs, weights, taps, rates, residues, skip):
    vmem = pl.BlockSpec(memory_space=pltpu.VMEM)
    smem = pl.BlockSpec(memory_space=pltpu.SMEM)
    return pl.pallas_call(
        front_kernel,
        out_shape=(
            jax.ShapeDtypeStruct((2 * BLOCK, LANES), F32),
            jax.ShapeDtypeStruct((2 * BLOCK, LANES), F32),
            jax.ShapeDtypeStruct((2 * SUB * MODES, LANES), F32),
            jax.ShapeDtypeStruct((CHIPS, EDGE_ROWS, LANES), F32),
        ),
        in_specs=[smem] + [vmem] * 10,
        out_specs=(vmem,) * 4,
        scratch_shapes=[
            pltpu.VMEM((2, 8 + BLOCK, WIDE), F32),
            pltpu.VMEM((2 * BLOCK, LANES), F32),
        ],
        compiler_params=pltpu.CompilerParams(vmem_limit_bytes=40 * 1024 * 1024),
        cost_estimate=pl.CostEstimate(
            flops=4 * BLOCK * 4096 * WIDE, bytes_accessed=6_000_000, transcendentals=0
        ),
    )(pos, slabs, *weights, taps, rates, residues, skip)


def back_kernel(
    pos, edges, sub_states, y_in, gate_in, rates, residues, skip, out, carried, mixed, head
):
    block = pos[0] * 4 + pos[1]
    rate = rates[...]
    weight = residues[...]
    decay = jnp.exp(-rate)
    long_decay = jnp.exp(-rate * float(STEPS))
    last = [jnp.exp(-rate * float(BLOCK - 1)), jnp.exp(-rate * float(BLOCK - 2))]

    def rows(chip, zh, start, count):
        return edges[chip, EDGE + 10 * zh + start : EDGE + 10 * zh + start + count, :]

    def late(chip, zh, tails):
        first, second = rows(chip, zh, 0, 2), rows(chip, zh, 2, 2)
        return (first + tails[0:2]) * (second + tails[2:4]) - first * second

    carry = [jnp.zeros((MODES, LANES), F32) for _ in range(2)]
    for other in range(CHIPS):
        distance = block - 1 - other
        span = jnp.maximum(distance, 0).astype(F32) * float(BLOCK)
        near = jnp.where(distance >= 0, jnp.exp(-rate * span), 0.0)
        far = jnp.exp(-rate * ((distance + CHIPS).astype(F32) * float(BLOCK)))
        states = []
        for zh in range(2):
            state = edges[other, zh * MODES : (zh + 1) * MODES, :]
            if other > 0 or zh == 1:
                ahead = (other - 1, zh) if other > 0 else (CHIPS - 1, 0)
                added = late(other, zh, rows(*ahead, 4, 4))
                state = state + last[0] * added[0:1] + last[1] * added[1:2]
            states.append(state)
        carry[0] = carry[0] + near * states[0]
        carry[1] = carry[1] + near * states[1] + far * states[0]
    decays = [jnp.broadcast_to(decay[m : m + 1], (SUB, LANES)) for m in range(MODES)]
    growth = jnp.exp(rate)
    gain = skip[...]
    ahead = jnp.maximum(block - 1, 0)
    for zh in range(2):
        tails = rows(ahead, zh, 4, 6)
        if zh == 0:
            tails = jnp.where(block == 0, 0.0, tails)
        else:
            tails = jnp.where(block == 0, rows(CHIPS - 1, 0, 4, 6), tails)
        added = late(block, zh, tails)
        state = carry[zh] + growth * (added[0:1] + growth * added[1:2])
        for sub in range(SUB):
            start = zh * SUB * MODES + sub * MODES
            carried[start : start + MODES, :] = weight * state
            state = long_decay * state + sub_states[start : start + MODES, :]
        terms = [
            carried[pl.ds(zh * SUB * MODES + m, SUB, stride=MODES), :] for m in range(MODES)
        ]
        for i in range(STEPS):
            at = pl.ds(zh * BLOCK + i, SUB, stride=STEPS)
            terms = [decays[m] * terms[m] for m in range(MODES)]
            sums = terms
            while len(sums) > 1:
                sums = [sums[k] + sums[k + 1] for k in range(0, len(sums), 2)]
            mixed[at, :] = y_in[at, :] + sums[0]
        early = jnp.sum(weight * growth, axis=0, keepdims=True) * added[1:2]
        start = zh * BLOCK
        mixed[start : start + 1, :] = mixed[start : start + 1, :] + gain * added[0:1] - early
        mixed[start + 1 : start + 2, :] = mixed[start + 1 : start + 2, :] + gain * added[1:2]
        head[...] = gate_in[start : start + 16, :]
        head[0:2, :] = head[0:2, :] + tails[4:6]
        for c in range(2):
            at = slice(start + c * HALF, start + (c + 1) * HALF)
            gate_rows = (gate_in[at, :] * mixed[at, :]).astype(BF16)
            for zl in range(4):
                out[(2 * zh + c) * 4 + zl] = gate_rows
        first_rows = (head[...] * mixed[start : start + 16, :]).astype(BF16)
        for zl in range(4):
            out[2 * zh * 4 + zl, 0:16, :] = first_rows


def back(pos, edges, sub_states, y, gate, rates, residues, skip):
    vmem = pl.BlockSpec(memory_space=pltpu.VMEM)
    smem = pl.BlockSpec(memory_space=pltpu.SMEM)
    return pl.pallas_call(
        back_kernel,
        out_shape=jax.ShapeDtypeStruct((16, HALF, LANES), BF16),
        in_specs=[smem] + [vmem] * 7,
        out_specs=vmem,
        scratch_shapes=[
            pltpu.VMEM((2 * SUB * MODES, LANES), F32),
            pltpu.VMEM((2 * BLOCK, LANES), F32),
            pltpu.VMEM((16, LANES), F32),
        ],
        compiler_params=pltpu.CompilerParams(vmem_limit_bytes=16 * 1024 * 1024),
        cost_estimate=pl.CostEstimate(
            flops=4_000_000, bytes_accessed=800_000, transcendentals=40_000
        ),
    )(pos, edges, sub_states, y, gate, rates, residues, skip)


def out_kernel(pos, gates, weights, out):
    own_zh = pos[2]
    total = jnp.zeros((HALF, 1024), F32)
    for k in range(2):
        for half in range(2):
            zl = (own_zh if k == 0 else 1 - own_zh) * 2 + half
            parts = [gates[(2 * zh + c) * 4 + zl] for zh in range(2) for c in range(2)]
            total = total + lax.dot_general(
                jnp.concatenate(parts, axis=1),
                weights[16 * half : 16 * (half + 1), k].reshape(1024, 512),
                (((1,), (1,)), ((), ())),
                preferred_element_type=F32,
            )
    out[...] = total.astype(BF16)


def project_out(pos, gates, weights):
    vmem = pl.BlockSpec(memory_space=pltpu.VMEM)
    smem = pl.BlockSpec(memory_space=pltpu.SMEM)
    return pl.pallas_call(
        out_kernel,
        out_shape=jax.ShapeDtypeStruct((HALF, 1024), BF16),
        in_specs=[smem, vmem, vmem],
        out_specs=vmem,
        compiler_params=pltpu.CompilerParams(vmem_limit_bytes=32 * 1024 * 1024),
        cost_estimate=pl.CostEstimate(
            flops=2 * HALF * 2048 * 1024, bytes_accessed=5_000_000, transcendentals=0
        ),
    )(pos, gates, weights)


def transposed_routes():
    near, far = [], []
    for zh, y, x, c, zl in np.ndindex(*SIZES):
        source = int(np.ravel_multi_index((zh, y, x, c, zl), SIZES))
        for route, to_zh in ((near, zl // 2), (far, 1 - zl // 2)):
            target = (to_zh, (zl % 2) * 2 + y % 2, x, c, zh * 2 + y // 2)
            route.append((source, int(np.ravel_multi_index(target, SIZES))))
    return near, far


def shards(tokens, in_weight, short_weight, residues, decay_rates, skip_gain, out_weight):
    zh, y, x, c = (lax.axis_index(axis) for axis in SEQ)
    pos = jnp.stack([y, x, zh, c]).astype(jnp.int32)
    group = zh * 2 + c

    slabs = lax.all_gather(tokens, ("zh", "zl", "c"), axis=0, tiled=False)
    slabs = slabs.reshape(2, 4, 2, HALF, 1024)

    quarters = in_weight.reshape(3, GROUP, 4, LANES).transpose(2, 1, 0, 3).reshape(4, GROUP, WIDE)

    def quarter(flip):
        part = lax.dynamic_index_in_dim(quarters, group ^ flip, 0, keepdims=False)
        if flip == 0:
            return part
        return lax.ppermute(part, ("zh", "c"), [(i, i ^ flip) for i in range(4)])

    def in_order(own, other):
        first = jnp.where(c == 0, own, other)
        second = jnp.where(c == 0, other, own)
        return jnp.concatenate([first, second], axis=0)

    far = in_order(quarter(2), quarter(3))
    near = in_order(quarter(0), quarter(1))
    gathered_once = jnp.concatenate(ring(jnp.concatenate([near, far], axis=0), 0), axis=0)
    in_weights = ring(gathered_once, 1)

    moved = [lax.ppermute(out_weight.T, AXES, route) for route in transposed_routes()]
    moved[0], moved[1], in_weights[1], in_weights[2] = lax.optimization_barrier(
        (moved[0], moved[1], in_weights[1], in_weights[2])
    )
    gathered = lax.all_gather(
        jnp.stack(moved),
        ("y", "x", "c"),
        axis=0,
        tiled=False,
    )

    def own_channels(table, axis):
        return lax.dynamic_slice_in_dim(table, group * LANES, LANES, axis)

    taps = own_channels(short_weight, 2).reshape(9, LANES)
    rates = own_channels(decay_rates, 0).T
    weights = own_channels(residues, 0).T
    skip = own_channels(skip_gain, 0)[None]
    mixed, gate, sub_states, edges = front(pos, slabs, in_weights, taps, rates, weights, skip)
    edges = lax.all_to_all(edges, ("y", "x"), split_axis=0, concat_axis=0, tiled=True)
    gate_out = back(pos, edges, sub_states, mixed, gate, rates, weights, skip)
    gates = lax.all_to_all(gate_out, ("zh", "c", "zl"), split_axis=0, concat_axis=0, tiled=True)
    return project_out(pos, gates, gathered)


def solution(mesh):
    split_mesh = Mesh(mesh.devices.reshape(SIZES), AXES)
    return jax.shard_map(
        shards,
        mesh=split_mesh,
        in_specs=(
            P(SEQ, "zl"),
            P(None, SEQ, "zl"),
            P(None, None, "zl"),
            P("zl", None),
            P("zl", None),
            P("zl"),
            P("zl", SEQ),
        ),
        out_specs=P(SEQ, "zl"),
        check_vma=False,
    )
```

```python
import functools

import jax
import jax.numpy as jnp
import numpy as np
from jax import lax
from jax.experimental import pallas as pl
from jax.experimental.pallas import tpu as pltpu
from jax.sharding import Mesh, PartitionSpec as P

AXES = ("zh", "yh", "yl", "x", "c", "zl")
SIZES = (2, 2, 2, 4, 2, 4)
SEQ = AXES[:5]
PLANE = ("yh", "yl", "x")
CHIPS = 16
BLOCK = 256
HALF = 128
LANES = 128
WIDE = 3 * LANES
MODES = 8
SUB = 8
STEPS = BLOCK // SUB
EDGE = 2 * MODES
EDGE_ROWS = 40
GROUP = 64
F32 = jnp.float32
BF16 = jnp.bfloat16


def crossed(block, phase, distance):
    route = []
    for y, x, c in np.ndindex(4, 4, 2):
        target = (y, (x + distance) % 4, c) if c == phase else ((y + distance) % 4, x, c)
        route.append((int(np.ravel_multi_index((y, x, c), (4, 4, 2))), int(np.ravel_multi_index(target, (4, 4, 2)))))
    return lax.ppermute(block, PLANE + ("c",), route)


def direct(block, phase):
    return [block] + [crossed(block, phase, distance) for distance in (1, -1, 2)]


RING_ORDER = (0, -1, 1, 2)


def front_kernel(
    pos,
    slabs,
    w0, w1, w2, w3, w4,
    taps,
    rates,
    residues,
    skip,
    y_out,
    gate_out,
    sub_out,
    edge_out,
    proj,
    gated,
):
    own_y, own_x, own_zh, own_c = pos[0], pos[1], pos[2], pos[3]

    def features(outer, inner, half):
        first = RING_ORDER[outer] + 4
        second = RING_ORDER[inner] + 4
        at_y = lax.rem(own_y + jnp.where(own_c == 0, first, second), 4)
        at_x = lax.rem(own_x + jnp.where(own_c == 0, second, first), 4)
        at_zh = own_zh if half == 0 else 1 - own_zh
        zl = at_zh * 2 + at_y // 2
        lane = pl.multiple_of((lax.rem(at_y, 2) * 4 + at_x) * 128, 128)
        return slabs[:, pl.ds(zl, 1), :, :, pl.ds(lane, 128)].reshape(2 * BLOCK, 128)

    total = None
    place = 0
    for array in (w0, w1, w2, w3, w4):
        count = array.shape[0] // 256
        parts = [
            features((place + k) // 4, (place + k) % 4, half)
            for k in range(count)
            for half in range(2)
        ]
        part = jnp.dot(jnp.concatenate(parts, axis=1), array[...], preferred_element_type=F32)
        total = part if total is None else total + part
        place += count
    proj[:, 0:8, :] = jnp.zeros((2, 8, WIDE), F32)
    proj[:, 8:, :] = total.astype(BF16).astype(F32).reshape(2, BLOCK, WIDE)
    gain = skip[...]
    for zh in range(2):
        streams = []
        edges = []
        for s in range(3):
            lanes = slice(s * LANES, (s + 1) * LANES)
            tap = [taps[3 * s + m : 3 * s + m + 1, :] for m in range(3)]
            total = jnp.zeros((BLOCK, LANES), F32)
            for m in range(3):
                total = total + tap[m] * proj[zh, 8 - m : 8 - m + BLOCK, lanes]
            streams.append(total)
            before = proj[zh, BLOCK + 6 : BLOCK + 7, lanes]
            last = proj[zh, BLOCK + 7 : BLOCK + 8, lanes]
            edges.append([tap[1] * last + tap[2] * before, tap[2] * last])
        gated[zh * BLOCK : (zh + 1) * BLOCK, :] = streams[0] * streams[2]
        gate_out[zh * BLOCK : (zh + 1) * BLOCK, :] = streams[1]
        rows = [streams[0][0:1], streams[0][1:2], streams[2][0:1], streams[2][1:2]]
        rows = rows + edges[0] + edges[2] + edges[1]
        for chip in range(CHIPS):
            for k, row in enumerate(rows):
                edge_out[chip, EDGE + zh * 10 + k : EDGE + zh * 10 + k + 1, :] = row
    rate = rates[...]
    decay = jnp.exp(-rate)
    weight = residues[...]
    decays = [jnp.broadcast_to(decay[m : m + 1], (SUB, LANES)) for m in range(MODES)]
    weights = [jnp.broadcast_to(weight[m : m + 1], (SUB, LANES)) for m in range(MODES)]
    gain = jnp.broadcast_to(gain, (SUB, LANES))
    long_decay = jnp.exp(-rate * float(STEPS))
    for zh in range(2):
        state = [jnp.zeros((SUB, LANES), F32) for _ in range(MODES)]
        for i in range(STEPS):
            rows = pl.ds(zh * BLOCK + i, SUB, stride=STEPS)
            entry = gated[rows, :]
            state = [decays[m] * state[m] + entry for m in range(MODES)]
            terms = [weights[m] * state[m] for m in range(MODES)]
            while len(terms) > 1:
                terms = [terms[k] + terms[k + 1] for k in range(0, len(terms), 2)]
            y_out[rows, :] = terms[0] + gain * entry
        for m in range(MODES):
            sub_out[pl.ds(zh * SUB * MODES + m, SUB, stride=MODES), :] = state[m]
        total = jnp.zeros((MODES, LANES), F32)
        for sub in range(SUB):
            start = zh * SUB * MODES + sub * MODES
            total = long_decay * total + sub_out[start : start + MODES, :]
        for chip in range(CHIPS):
            edge_out[chip, zh * MODES : (zh + 1) * MODES, :] = total


def front(pos, slabs, weights, taps, rates, residues, skip):
    vmem = pl.BlockSpec(memory_space=pltpu.VMEM)
    smem = pl.BlockSpec(memory_space=pltpu.SMEM)
    return pl.pallas_call(
        front_kernel,
        out_shape=(
            jax.ShapeDtypeStruct((2 * BLOCK, LANES), F32),
            jax.ShapeDtypeStruct((2 * BLOCK, LANES), F32),
            jax.ShapeDtypeStruct((2 * SUB * MODES, LANES), F32),
            jax.ShapeDtypeStruct((CHIPS, EDGE_ROWS, LANES), F32),
        ),
        in_specs=[smem] + [vmem] * 10,
        out_specs=(vmem,) * 4,
        scratch_shapes=[
            pltpu.VMEM((2, 8 + BLOCK, WIDE), F32),
            pltpu.VMEM((2 * BLOCK, LANES), F32),
        ],
        compiler_params=pltpu.CompilerParams(vmem_limit_bytes=40 * 1024 * 1024),
        cost_estimate=pl.CostEstimate(
            flops=4 * BLOCK * 4096 * WIDE, bytes_accessed=6_000_000, transcendentals=0
        ),
    )(pos, slabs, *weights, taps, rates, residues, skip)


def back_kernel(
    pos, edges, sub_states, y_in, gate_in, rates, residues, skip, out, carried, mixed, head
):
    block = pos[0] * 4 + pos[1]
    rate = rates[...]
    weight = residues[...]
    decay = jnp.exp(-rate)
    long_decay = jnp.exp(-rate * float(STEPS))
    last = [jnp.exp(-rate * float(BLOCK - 1)), jnp.exp(-rate * float(BLOCK - 2))]

    def rows(chip, zh, start, count):
        return edges[chip, EDGE + 10 * zh + start : EDGE + 10 * zh + start + count, :]

    def late(chip, zh, tails):
        first, second = rows(chip, zh, 0, 2), rows(chip, zh, 2, 2)
        return (first + tails[0:2]) * (second + tails[2:4]) - first * second

    carry = [jnp.zeros((MODES, LANES), F32) for _ in range(2)]
    for other in range(CHIPS):
        distance = block - 1 - other
        span = jnp.maximum(distance, 0).astype(F32) * float(BLOCK)
        near = jnp.where(distance >= 0, jnp.exp(-rate * span), 0.0)
        far = jnp.exp(-rate * ((distance + CHIPS).astype(F32) * float(BLOCK)))
        states = []
        for zh in range(2):
            state = edges[other, zh * MODES : (zh + 1) * MODES, :]
            if other > 0 or zh == 1:
                ahead = (other - 1, zh) if other > 0 else (CHIPS - 1, 0)
                added = late(other, zh, rows(*ahead, 4, 4))
                state = state + last[0] * added[0:1] + last[1] * added[1:2]
            states.append(state)
        carry[0] = carry[0] + near * states[0]
        carry[1] = carry[1] + near * states[1] + far * states[0]
    decays = [jnp.broadcast_to(decay[m : m + 1], (SUB, LANES)) for m in range(MODES)]
    growth = jnp.exp(rate)
    gain = skip[...]
    ahead = jnp.maximum(block - 1, 0)
    for zh in range(2):
        tails = rows(ahead, zh, 4, 6)
        if zh == 0:
            tails = jnp.where(block == 0, 0.0, tails)
        else:
            tails = jnp.where(block == 0, rows(CHIPS - 1, 0, 4, 6), tails)
        added = late(block, zh, tails)
        state = carry[zh] + growth * (added[0:1] + growth * added[1:2])
        for sub in range(SUB):
            start = zh * SUB * MODES + sub * MODES
            carried[start : start + MODES, :] = weight * state
            state = long_decay * state + sub_states[start : start + MODES, :]
        terms = [
            carried[pl.ds(zh * SUB * MODES + m, SUB, stride=MODES), :] for m in range(MODES)
        ]
        for i in range(STEPS):
            at = pl.ds(zh * BLOCK + i, SUB, stride=STEPS)
            terms = [decays[m] * terms[m] for m in range(MODES)]
            sums = terms
            while len(sums) > 1:
                sums = [sums[k] + sums[k + 1] for k in range(0, len(sums), 2)]
            mixed[at, :] = y_in[at, :] + sums[0]
        early = jnp.sum(weight * growth, axis=0, keepdims=True) * added[1:2]
        start = zh * BLOCK
        mixed[start : start + 1, :] = mixed[start : start + 1, :] + gain * added[0:1] - early
        mixed[start + 1 : start + 2, :] = mixed[start + 1 : start + 2, :] + gain * added[1:2]
        head[...] = gate_in[start : start + 16, :]
        head[0:2, :] = head[0:2, :] + tails[4:6]
        for c in range(2):
            at = slice(start + c * HALF, start + (c + 1) * HALF)
            gate_rows = (gate_in[at, :] * mixed[at, :]).astype(BF16)
            for zl in range(4):
                out[(2 * zh + c) * 4 + zl] = gate_rows
        first_rows = (head[...] * mixed[start : start + 16, :]).astype(BF16)
        for zl in range(4):
            out[2 * zh * 4 + zl, 0:16, :] = first_rows


def back(pos, edges, sub_states, y, gate, rates, residues, skip):
    vmem = pl.BlockSpec(memory_space=pltpu.VMEM)
    smem = pl.BlockSpec(memory_space=pltpu.SMEM)
    return pl.pallas_call(
        back_kernel,
        out_shape=jax.ShapeDtypeStruct((16, HALF, LANES), BF16),
        in_specs=[smem] + [vmem] * 7,
        out_specs=vmem,
        scratch_shapes=[
            pltpu.VMEM((2 * SUB * MODES, LANES), F32),
            pltpu.VMEM((2 * BLOCK, LANES), F32),
            pltpu.VMEM((16, LANES), F32),
        ],
        compiler_params=pltpu.CompilerParams(vmem_limit_bytes=16 * 1024 * 1024),
        cost_estimate=pl.CostEstimate(
            flops=4_000_000, bytes_accessed=800_000, transcendentals=40_000
        ),
    )(pos, edges, sub_states, y, gate, rates, residues, skip)


def out_kernel(pos, gates, weights, out):
    own_zh, own_yh = pos[2], pos[0] // 2
    total = jnp.zeros((HALF, 1024), F32)
    for depth in range(2):
        for flip in range(2):
            high = own_zh if depth == 0 else 1 - own_zh
            zl = high * 2 + (own_yh if flip == 0 else 1 - own_yh)
            left = [gates[(2 * zh + c) * 4 + zl] for zh in range(2) for c in range(2)]
            right = [
                weights[x, yl, c, flip, depth]
                for yl in range(2)
                for x in range(4)
                for c in range(2)
            ]
            total = total + lax.dot_general(
                jnp.concatenate(left, axis=1),
                jnp.concatenate(right, axis=0),
                (((1,), (1,)), ((), ())),
                preferred_element_type=F32,
            )
    out[...] = total.astype(BF16)


def project_out(pos, gates, weights):
    vmem = pl.BlockSpec(memory_space=pltpu.VMEM)
    smem = pl.BlockSpec(memory_space=pltpu.SMEM)
    return pl.pallas_call(
        out_kernel,
        out_shape=jax.ShapeDtypeStruct((HALF, 1024), BF16),
        in_specs=[smem, vmem, vmem],
        out_specs=vmem,
        compiler_params=pltpu.CompilerParams(vmem_limit_bytes=32 * 1024 * 1024),
        cost_estimate=pl.CostEstimate(
            flops=2 * HALF * 2048 * 1024, bytes_accessed=5_000_000, transcendentals=0
        ),
    )(pos, gates, weights)


def transposed_routes():
    routes = [[], []]
    for zh, yh, yl, x, c, zl in np.ndindex(*SIZES):
        source = int(np.ravel_multi_index((zh, yh, yl, x, c, zl), SIZES))
        for flip in range(2):
            target = ((zl // 2) ^ flip, zl % 2, yl, x, c, zh * 2 + yh)
            routes[flip].append((source, int(np.ravel_multi_index(target, SIZES))))
    return routes


def shards(tokens, in_weight, short_weight, residues, decay_rates, skip_gain, out_weight):
    zh, x, c = (lax.axis_index(axis) for axis in ("zh", "x", "c"))
    y = lax.axis_index(("yh", "yl"))
    pos = jnp.stack([y, x, zh, c]).astype(jnp.int32)
    group = zh * 2 + c

    slabs = lax.all_gather(tokens, ("zh", "zl", "c"), axis=0, tiled=False)
    slabs = slabs.reshape(2, 4, 2, HALF, 1024)

    quarters = in_weight.reshape(3, GROUP, 4, LANES).transpose(2, 1, 0, 3).reshape(4, GROUP, WIDE)

    def quarter(flip):
        part = lax.dynamic_index_in_dim(quarters, group ^ flip, 0, keepdims=False)
        if flip == 0:
            return part
        return lax.ppermute(part, ("zh", "c"), [(i, i ^ flip) for i in range(4)])

    def in_order(own, other):
        first = jnp.where(c == 0, own, other)
        second = jnp.where(c == 0, other, own)
        return jnp.concatenate([first, second], axis=0)

    far = in_order(quarter(2), quarter(3))
    near = in_order(quarter(0), quarter(1))
    gathered_once = jnp.concatenate(direct(jnp.concatenate([near, far], axis=0), 0), axis=0)

    half = gathered_once.shape[0] // 2
    low = crossed(gathered_once, 1, 1)
    high = crossed(gathered_once, 1, -1)
    moved = [lax.ppermute(out_weight.T, AXES, route) for route in transposed_routes()]
    low, high, moved = lax.optimization_barrier((low, high, moved))
    moved = jnp.concatenate(moved, axis=0)
    far_low = crossed(low[:half], 1, 1)
    far_high = crossed(high[half:], 1, -1)
    flipped = lax.ppermute(moved, "yh", [(0, 1), (1, 0)])
    far_low, far_high, flipped = lax.optimization_barrier((far_low, far_high, flipped))
    in_weights = [gathered_once, low, high, far_low, far_high]

    slabs, in_weights[3] = lax.optimization_barrier((slabs, in_weights[3]))

    gathered = lax.all_gather(jnp.stack([moved, flipped]), ("x", "yl", "c"), axis=0, tiled=False)
    gathered = gathered.reshape(4, 2, 2, 2, 2, GROUP, 512)

    def own_channels(table, axis):
        return lax.dynamic_slice_in_dim(table, group * LANES, LANES, axis)

    taps = own_channels(short_weight, 2).reshape(9, LANES)
    rates = own_channels(decay_rates, 0).T
    weights = own_channels(residues, 0).T
    skip = own_channels(skip_gain, 0)[None]
    mixed, gate, sub_states, edges = front(pos, slabs, in_weights, taps, rates, weights, skip)
    edges = lax.all_to_all(edges, PLANE, split_axis=0, concat_axis=0, tiled=True)
    gate_out = back(pos, edges, sub_states, mixed, gate, rates, weights, skip)
    gates = lax.all_to_all(gate_out, ("zh", "c", "zl"), split_axis=0, concat_axis=0, tiled=True)
    return project_out(pos, gates, gathered)


def solution(mesh):
    split_mesh = Mesh(mesh.devices.reshape(SIZES), AXES)
    return jax.shard_map(
        shards,
        mesh=split_mesh,
        in_specs=(
            P(SEQ, "zl"),
            P(None, SEQ, "zl"),
            P(None, None, "zl"),
            P("zl", None),
            P("zl", None),
            P("zl"),
            P("zl", SEQ),
        ),
        out_specs=P(SEQ, "zl"),
        check_vma=False,
    )
```

```python
import functools

import jax
import jax.numpy as jnp
import numpy as np
from jax import lax
from jax.experimental import pallas as pl
from jax.experimental.pallas import tpu as pltpu
from jax.sharding import Mesh, PartitionSpec as P

AXES = ("zh", "yh", "yl", "x", "c", "zl")
SIZES = (2, 2, 2, 4, 2, 4)
SEQ = AXES[:5]
PLANE = ("yh", "yl", "x")
CHIPS = 16
BLOCK = 256
HALF = 128
LANES = 128
WIDE = 3 * LANES
MODES = 8
SUB = 8
STEPS = BLOCK // SUB
EDGE = 2 * MODES
EDGE_ROWS = 40
GROUP = 64
F32 = jnp.float32
BF16 = jnp.bfloat16


def crossed(block, phase, distance):
    route = []
    for y, x, c in np.ndindex(4, 4, 2):
        target = (y, (x + distance) % 4, c) if c != phase else ((y + distance) % 4, x, c)
        route.append((int(np.ravel_multi_index((y, x, c), (4, 4, 2))), int(np.ravel_multi_index(target, (4, 4, 2)))))
    return lax.ppermute(block, PLANE + ("c",), route)


def direct(block, phase):
    return [block] + [crossed(block, phase, distance) for distance in (1, -1, 2)]


RING_ORDER = (0, -1, 1, 2)


def front_kernel(
    pos,
    slabs,
    w0, w1, w2, w3, w4,
    taps,
    rates,
    residues,
    skip,
    y_out,
    gate_out,
    sub_out,
    edge_out,
    proj,
    gated,
):
    own_y, own_x, own_zh, own_c = pos[0], pos[1], pos[2], pos[3]

    def features(outer, inner, half):
        first = RING_ORDER[outer] + 4
        second = RING_ORDER[inner] + 4
        at_y = lax.rem(own_y + jnp.where(own_c == 1, first, second), 4)
        at_x = lax.rem(own_x + jnp.where(own_c == 1, second, first), 4)
        at_zh = own_zh if half == 0 else 1 - own_zh
        zl = at_zh * 2 + at_y // 2
        lane = pl.multiple_of((lax.rem(at_y, 2) * 4 + at_x) * 128, 128)
        return slabs[:, pl.ds(zl, 1), :, :, pl.ds(lane, 128)].reshape(2 * BLOCK, 128)

    total = None
    place = 0
    for array in (w0, w1, w2, w3, w4):
        count = array.shape[0] // 256
        parts = [
            features((place + k) // 4, (place + k) % 4, half)
            for k in range(count)
            for half in range(2)
        ]
        part = jnp.dot(jnp.concatenate(parts, axis=1), array[...], preferred_element_type=F32)
        total = part if total is None else total + part
        place += count
    proj[:, 0:8, :] = jnp.zeros((2, 8, WIDE), F32)
    proj[:, 8:, :] = total.astype(BF16).astype(F32).reshape(2, BLOCK, WIDE)
    gain = skip[...]
    for zh in range(2):
        streams = []
        edges = []
        for s in range(3):
            lanes = slice(s * LANES, (s + 1) * LANES)
            tap = [taps[3 * s + m : 3 * s + m + 1, :] for m in range(3)]
            total = jnp.zeros((BLOCK, LANES), F32)
            for m in range(3):
                total = total + tap[m] * proj[zh, 8 - m : 8 - m + BLOCK, lanes]
            streams.append(total)
            before = proj[zh, BLOCK + 6 : BLOCK + 7, lanes]
            last = proj[zh, BLOCK + 7 : BLOCK + 8, lanes]
            edges.append([tap[1] * last + tap[2] * before, tap[2] * last])
        gated[zh * BLOCK : (zh + 1) * BLOCK, :] = streams[0] * streams[2]
        gate_out[zh * BLOCK : (zh + 1) * BLOCK, :] = streams[1]
        rows = [streams[0][0:1], streams[0][1:2], streams[2][0:1], streams[2][1:2]]
        rows = rows + edges[0] + edges[2] + edges[1]
        for chip in range(CHIPS):
            for k, row in enumerate(rows):
                edge_out[chip, EDGE + zh * 10 + k : EDGE + zh * 10 + k + 1, :] = row
    rate = rates[...]
    decay = jnp.exp(-rate)
    weight = residues[...]
    decays = [jnp.broadcast_to(decay[m : m + 1], (SUB, LANES)) for m in range(MODES)]
    weights = [jnp.broadcast_to(weight[m : m + 1], (SUB, LANES)) for m in range(MODES)]
    gain = jnp.broadcast_to(gain, (SUB, LANES))
    long_decay = jnp.exp(-rate * float(STEPS))
    for zh in range(2):
        state = [jnp.zeros((SUB, LANES), F32) for _ in range(MODES)]
        for i in range(STEPS):
            rows = pl.ds(zh * BLOCK + i, SUB, stride=STEPS)
            entry = gated[rows, :]
            state = [decays[m] * state[m] + entry for m in range(MODES)]
            terms = [weights[m] * state[m] for m in range(MODES)]
            while len(terms) > 1:
                terms = [terms[k] + terms[k + 1] for k in range(0, len(terms), 2)]
            y_out[rows, :] = terms[0] + gain * entry
        for m in range(MODES):
            sub_out[pl.ds(zh * SUB * MODES + m, SUB, stride=MODES), :] = state[m]
        total = jnp.zeros((MODES, LANES), F32)
        for sub in range(SUB):
            start = zh * SUB * MODES + sub * MODES
            total = long_decay * total + sub_out[start : start + MODES, :]
        for chip in range(CHIPS):
            edge_out[chip, zh * MODES : (zh + 1) * MODES, :] = total


def front(pos, slabs, weights, taps, rates, residues, skip):
    vmem = pl.BlockSpec(memory_space=pltpu.VMEM)
    smem = pl.BlockSpec(memory_space=pltpu.SMEM)
    return pl.pallas_call(
        front_kernel,
        out_shape=(
            jax.ShapeDtypeStruct((2 * BLOCK, LANES), F32),
            jax.ShapeDtypeStruct((2 * BLOCK, LANES), F32),
            jax.ShapeDtypeStruct((2 * SUB * MODES, LANES), F32),
            jax.ShapeDtypeStruct((CHIPS, EDGE_ROWS, LANES), F32),
        ),
        in_specs=[smem] + [vmem] * 10,
        out_specs=(vmem,) * 4,
        scratch_shapes=[
            pltpu.VMEM((2, 8 + BLOCK, WIDE), F32),
            pltpu.VMEM((2 * BLOCK, LANES), F32),
        ],
        compiler_params=pltpu.CompilerParams(vmem_limit_bytes=40 * 1024 * 1024),
        cost_estimate=pl.CostEstimate(
            flops=4 * BLOCK * 4096 * WIDE, bytes_accessed=6_000_000, transcendentals=0
        ),
    )(pos, slabs, *weights, taps, rates, residues, skip)


def back_kernel(
    pos, edges, sub_states, y_in, gate_in, rates, residues, skip, out, carried, mixed, head
):
    block = pos[0] * 4 + pos[1]
    rate = rates[...]
    weight = residues[...]
    decay = jnp.exp(-rate)
    long_decay = jnp.exp(-rate * float(STEPS))
    last = [jnp.exp(-rate * float(BLOCK - 1)), jnp.exp(-rate * float(BLOCK - 2))]

    def rows(chip, zh, start, count):
        return edges[chip, EDGE + 10 * zh + start : EDGE + 10 * zh + start + count, :]

    def late(chip, zh, tails):
        first, second = rows(chip, zh, 0, 2), rows(chip, zh, 2, 2)
        return (first + tails[0:2]) * (second + tails[2:4]) - first * second

    carry = [jnp.zeros((MODES, LANES), F32) for _ in range(2)]
    for other in range(CHIPS):
        distance = block - 1 - other
        span = jnp.maximum(distance, 0).astype(F32) * float(BLOCK)
        near = jnp.where(distance >= 0, jnp.exp(-rate * span), 0.0)
        far = jnp.exp(-rate * ((distance + CHIPS).astype(F32) * float(BLOCK)))
        states = []
        for zh in range(2):
            state = edges[other, zh * MODES : (zh + 1) * MODES, :]
            if other > 0 or zh == 1:
                ahead = (other - 1, zh) if other > 0 else (CHIPS - 1, 0)
                added = late(other, zh, rows(*ahead, 4, 4))
                state = state + last[0] * added[0:1] + last[1] * added[1:2]
            states.append(state)
        carry[0] = carry[0] + near * states[0]
        carry[1] = carry[1] + near * states[1] + far * states[0]
    decays = [jnp.broadcast_to(decay[m : m + 1], (SUB, LANES)) for m in range(MODES)]
    growth = jnp.exp(rate)
    gain = skip[...]
    ahead = jnp.maximum(block - 1, 0)
    for zh in range(2):
        tails = rows(ahead, zh, 4, 6)
        if zh == 0:
            tails = jnp.where(block == 0, 0.0, tails)
        else:
            tails = jnp.where(block == 0, rows(CHIPS - 1, 0, 4, 6), tails)
        added = late(block, zh, tails)
        state = carry[zh] + growth * (added[0:1] + growth * added[1:2])
        for sub in range(SUB):
            start = zh * SUB * MODES + sub * MODES
            carried[start : start + MODES, :] = weight * state
            state = long_decay * state + sub_states[start : start + MODES, :]
        terms = [
            carried[pl.ds(zh * SUB * MODES + m, SUB, stride=MODES), :] for m in range(MODES)
        ]
        for i in range(STEPS):
            at = pl.ds(zh * BLOCK + i, SUB, stride=STEPS)
            terms = [decays[m] * terms[m] for m in range(MODES)]
            sums = terms
            while len(sums) > 1:
                sums = [sums[k] + sums[k + 1] for k in range(0, len(sums), 2)]
            mixed[at, :] = y_in[at, :] + sums[0]
        early = jnp.sum(weight * growth, axis=0, keepdims=True) * added[1:2]
        start = zh * BLOCK
        mixed[start : start + 1, :] = mixed[start : start + 1, :] + gain * added[0:1] - early
        mixed[start + 1 : start + 2, :] = mixed[start + 1 : start + 2, :] + gain * added[1:2]
        head[...] = gate_in[start : start + 16, :]
        head[0:2, :] = head[0:2, :] + tails[4:6]
        for c in range(2):
            at = slice(start + c * HALF, start + (c + 1) * HALF)
            gate_rows = (gate_in[at, :] * mixed[at, :]).astype(BF16)
            for zl in range(4):
                out[(2 * zh + c) * 4 + zl] = gate_rows
        first_rows = (head[...] * mixed[start : start + 16, :]).astype(BF16)
        for zl in range(4):
            out[2 * zh * 4 + zl, 0:16, :] = first_rows


def back(pos, edges, sub_states, y, gate, rates, residues, skip):
    vmem = pl.BlockSpec(memory_space=pltpu.VMEM)
    smem = pl.BlockSpec(memory_space=pltpu.SMEM)
    return pl.pallas_call(
        back_kernel,
        out_shape=jax.ShapeDtypeStruct((16, HALF, LANES), BF16),
        in_specs=[smem] + [vmem] * 7,
        out_specs=vmem,
        scratch_shapes=[
            pltpu.VMEM((2 * SUB * MODES, LANES), F32),
            pltpu.VMEM((2 * BLOCK, LANES), F32),
            pltpu.VMEM((16, LANES), F32),
        ],
        compiler_params=pltpu.CompilerParams(vmem_limit_bytes=16 * 1024 * 1024),
        cost_estimate=pl.CostEstimate(
            flops=4_000_000, bytes_accessed=800_000, transcendentals=40_000
        ),
    )(pos, edges, sub_states, y, gate, rates, residues, skip)


def out_kernel(pos, gates, weights, out):
    own_zh, own_yh = pos[2], pos[0] // 2
    total = jnp.zeros((HALF, 1024), F32)
    for depth in range(2):
        for flip in range(2):
            high = own_zh if depth == 0 else 1 - own_zh
            zl = high * 2 + (own_yh if flip == 0 else 1 - own_yh)
            left = [gates[(2 * zh + c) * 4 + zl] for zh in range(2) for c in range(2)]
            right = [
                weights[x, yl, c, flip, depth]
                for yl in range(2)
                for x in range(4)
                for c in range(2)
            ]
            total = total + lax.dot_general(
                jnp.concatenate(left, axis=1),
                jnp.concatenate(right, axis=0),
                (((1,), (1,)), ((), ())),
                preferred_element_type=F32,
            )
    out[...] = total.astype(BF16)


def project_out(pos, gates, weights):
    vmem = pl.BlockSpec(memory_space=pltpu.VMEM)
    smem = pl.BlockSpec(memory_space=pltpu.SMEM)
    return pl.pallas_call(
        out_kernel,
        out_shape=jax.ShapeDtypeStruct((HALF, 1024), BF16),
        in_specs=[smem, vmem, vmem],
        out_specs=vmem,
        compiler_params=pltpu.CompilerParams(vmem_limit_bytes=32 * 1024 * 1024),
        cost_estimate=pl.CostEstimate(
            flops=2 * HALF * 2048 * 1024, bytes_accessed=5_000_000, transcendentals=0
        ),
    )(pos, gates, weights)


def split_kernel(weight, *parts):
    group = lax.axis_index("zh") * 2 + lax.axis_index("c")
    for flip, part in enumerate(parts):
        lane = pl.multiple_of((group ^ flip) * LANES, LANES)
        for s in range(3):
            part[:, s * LANES : (s + 1) * LANES] = weight[s, :, pl.ds(lane, LANES)]


def split(in_weight):
    vmem = pl.BlockSpec(memory_space=pltpu.VMEM)
    return pl.pallas_call(
        split_kernel,
        out_shape=(jax.ShapeDtypeStruct((GROUP, WIDE), BF16),) * 4,
        in_specs=[vmem],
        out_specs=(vmem,) * 4,
        compiler_params=pltpu.CompilerParams(vmem_limit_bytes=8 * 1024 * 1024),
    )(in_weight)


def transposed_routes():
    routes = [[], []]
    for zh, yh, yl, x, c, zl in np.ndindex(*SIZES):
        source = int(np.ravel_multi_index((zh, yh, yl, x, c, zl), SIZES))
        for flip in range(2):
            target = ((zl // 2) ^ flip, zl % 2, yl, x, c, zh * 2 + yh)
            routes[flip].append((source, int(np.ravel_multi_index(target, SIZES))))
    return routes


def shards(tokens, in_weight, short_weight, residues, decay_rates, skip_gain, out_weight):
    zh, x, c = (lax.axis_index(axis) for axis in ("zh", "x", "c"))
    y = lax.axis_index(("yh", "yl"))
    pos = jnp.stack([y, x, zh, c]).astype(jnp.int32)
    group = zh * 2 + c

    slabs = lax.all_gather(tokens, ("zh", "zl", "c"), axis=0, tiled=False)
    slabs = slabs.reshape(2, 4, 2, HALF, 1024)

    quarters = split(in_weight)

    def quarter(flip):
        if flip == 0:
            return quarters[0]
        return lax.ppermute(quarters[flip], ("zh", "c"), [(i, i ^ flip) for i in range(4)])

    def in_order(own, other):
        first = jnp.where(c == 0, own, other)
        second = jnp.where(c == 0, other, own)
        return jnp.concatenate([first, second], axis=0)

    far = in_order(quarter(2), quarter(3))
    near = in_order(quarter(0), quarter(1))
    gathered_once = jnp.concatenate(direct(jnp.concatenate([near, far], axis=0), 0), axis=0)

    def own_channels(table, axis):
        return lax.dynamic_slice_in_dim(table, group * LANES, LANES, axis)

    taps = own_channels(short_weight, 2).reshape(9, LANES)
    rates = own_channels(decay_rates, 0).T
    weights = own_channels(residues, 0).T
    skip = own_channels(skip_gain, 0)[None]

    half = gathered_once.shape[0] // 2
    low = crossed(gathered_once, 1, 1)
    high = crossed(gathered_once, 1, -1)
    moved = [lax.ppermute(out_weight.T, AXES, route) for route in transposed_routes()]
    tables = (pos, taps, rates, weights, skip)
    low, high, moved, tables = lax.optimization_barrier((low, high, moved, tables))
    pos, taps, rates, weights, skip = tables
    moved = jnp.concatenate(moved, axis=0)
    far_low = crossed(low[:half], 1, 1)
    far_high = crossed(high[half:], 1, -1)
    flipped = lax.ppermute(moved, "yh", [(0, 1), (1, 0)])
    far_low, far_high, slabs = lax.optimization_barrier((far_low, far_high, slabs))
    far_low, far_high, flipped = lax.optimization_barrier((far_low, far_high, flipped))
    in_weights = [gathered_once, low, high, far_low, far_high]

    slabs, in_weights[3] = lax.optimization_barrier((slabs, in_weights[3]))

    gathered = lax.all_gather(jnp.stack([moved, flipped]), ("x", "yl", "c"), axis=0, tiled=False)
    gathered = gathered.reshape(4, 2, 2, 2, 2, GROUP, 512)

    mixed, gate, sub_states, edges = front(pos, slabs, in_weights, taps, rates, weights, skip)
    edges = lax.all_to_all(edges, PLANE, split_axis=0, concat_axis=0, tiled=True)
    gate_out = back(pos, edges, sub_states, mixed, gate, rates, weights, skip)
    gates = lax.all_to_all(gate_out, ("zh", "c", "zl"), split_axis=0, concat_axis=0, tiled=True)
    return project_out(pos, gates, gathered)


def solution(mesh):
    split_mesh = Mesh(mesh.devices.reshape(SIZES), AXES)
    return jax.shard_map(
        shards,
        mesh=split_mesh,
        in_specs=(
            P(SEQ, "zl"),
            P(None, SEQ, "zl"),
            P(None, None, "zl"),
            P("zl", None),
            P("zl", None),
            P("zl"),
            P("zl", SEQ),
        ),
        out_specs=P(SEQ, "zl"),
        check_vma=False,
    )
```

```python
import functools

import jax
import jax.numpy as jnp
import numpy as np
from jax import lax
from jax.experimental import pallas as pl
from jax.experimental.pallas import tpu as pltpu
from jax.sharding import Mesh, PartitionSpec as P

AXES = ("zh", "yh", "yl", "x", "c", "zl")
SIZES = (2, 2, 2, 4, 2, 4)
SEQ = AXES[:5]
PLANE = ("yh", "yl", "x")
CHIPS = 16
BLOCK = 256
HALF = 128
LANES = 128
WIDE = 3 * LANES
MODES = 8
SUB = 8
STEPS = BLOCK // SUB
EDGE = 4 * MODES
EDGE_ROWS = 56
GROUP = 64
F32 = jnp.float32
BF16 = jnp.bfloat16


def crossed(block, phase, distance):
    route = []
    for y, x, c in np.ndindex(4, 4, 2):
        target = (y, (x + distance) % 4, c) if c != phase else ((y + distance) % 4, x, c)
        route.append((int(np.ravel_multi_index((y, x, c), (4, 4, 2))), int(np.ravel_multi_index(target, (4, 4, 2)))))
    return lax.ppermute(block, PLANE + ("c",), route)


def direct(block, phase):
    return [block] + [crossed(block, phase, distance) for distance in (1, -1, 2)]


RING_ORDER = (0, -1, 1, 2)


def front_kernel(
    pos,
    slabs,
    w0, w1, w2, w3, w4,
    taps,
    rates,
    residues,
    skip,
    y_out,
    gate_out,
    sub_out,
    edge_out,
    proj,
    gated,
    edge,
):
    own_y, own_x, own_zh, own_c = pos[0], pos[1], pos[2], pos[3]

    def features(outer, inner, half):
        first = RING_ORDER[outer] + 4
        second = RING_ORDER[inner] + 4
        at_y = lax.rem(own_y + jnp.where(own_c == 1, first, second), 4)
        at_x = lax.rem(own_x + jnp.where(own_c == 1, second, first), 4)
        at_zh = own_zh if half == 0 else 1 - own_zh
        zl = at_zh * 2 + at_y // 2
        lane = pl.multiple_of((lax.rem(at_y, 2) * 4 + at_x) * 128, 128)
        return slabs[:, pl.ds(zl, 1), :, :, pl.ds(lane, 128)].reshape(2 * BLOCK, 128)

    total = None
    place = 0
    for array in (w0, w1, w2, w3, w4):
        count = array.shape[0] // 256
        parts = [
            features((place + k) // 4, (place + k) % 4, half)
            for k in range(count)
            for half in range(2)
        ]
        part = jnp.dot(jnp.concatenate(parts, axis=1), array[...], preferred_element_type=F32)
        total = part if total is None else total + part
        place += count
    proj[:, 0:8, :] = jnp.zeros((2, 8, WIDE), F32)
    proj[:, 8:, :] = total.astype(BF16).astype(F32).reshape(2, BLOCK, WIDE)
    gain = skip[...]
    for zh in range(2):
        streams = []
        for s in range(3):
            lanes = slice(s * LANES, (s + 1) * LANES)
            tap = [taps[3 * s + m : 3 * s + m + 1, :] for m in range(3)]
            total = jnp.zeros((BLOCK, LANES), F32)
            for m in range(3):
                total = total + tap[m] * proj[zh, 8 - m : 8 - m + BLOCK, lanes]
            streams.append(total)
        gated[zh * BLOCK : (zh + 1) * BLOCK, :] = streams[0] * streams[2]
        gate_out[zh * BLOCK : (zh + 1) * BLOCK, :] = streams[1]
        for k, (s, row) in enumerate(((0, 8), (2, 8), (0, -2), (2, -2), (1, -2))):
            row = row if row > 0 else 8 + BLOCK + row
            start = EDGE + 10 * zh + 2 * k
            edge[start : start + 2, :] = proj[zh, row : row + 2, s * LANES : (s + 1) * LANES]
    edge[EDGE + 20 :, :] = jnp.zeros((EDGE_ROWS - EDGE - 20, LANES), F32)
    rate = rates[...]
    decay = jnp.exp(-rate)
    weight = residues[...]
    decays = [jnp.broadcast_to(decay[m : m + 1], (SUB, LANES)) for m in range(MODES)]
    weights = [jnp.broadcast_to(weight[m : m + 1], (SUB, LANES)) for m in range(MODES)]
    gain = jnp.broadcast_to(gain, (SUB, LANES))
    long_decay = jnp.exp(-rate * float(STEPS))
    for zh in range(2):
        state = [jnp.zeros((SUB, LANES), F32) for _ in range(MODES)]
        for i in range(STEPS):
            rows = pl.ds(zh * BLOCK + i, SUB, stride=STEPS)
            entry = gated[rows, :]
            state = [decays[m] * state[m] + entry for m in range(MODES)]
            terms = [weights[m] * state[m] for m in range(MODES)]
            while len(terms) > 1:
                terms = [terms[k] + terms[k + 1] for k in range(0, len(terms), 2)]
            y_out[rows, :] = terms[0] + gain * entry
        for m in range(MODES):
            sub_out[pl.ds(zh * SUB * MODES + m, SUB, stride=MODES), :] = state[m]
        total = jnp.zeros((MODES, LANES), F32)
        for sub in range(SUB):
            start = zh * SUB * MODES + sub * MODES
            total = long_decay * total + sub_out[start : start + MODES, :]
        upper = total.astype(BF16).astype(F32)
        edge[zh * MODES : (zh + 1) * MODES, :] = upper
        edge[(2 + zh) * MODES : (3 + zh) * MODES, :] = total - upper
    sent = edge[...].astype(BF16)
    for chip in range(CHIPS):
        edge_out[chip] = sent


def front(pos, slabs, weights, taps, rates, residues, skip):
    vmem = pl.BlockSpec(memory_space=pltpu.VMEM)
    smem = pl.BlockSpec(memory_space=pltpu.SMEM)
    return pl.pallas_call(
        front_kernel,
        out_shape=(
            jax.ShapeDtypeStruct((2 * BLOCK, LANES), F32),
            jax.ShapeDtypeStruct((2 * BLOCK, LANES), F32),
            jax.ShapeDtypeStruct((2 * SUB * MODES, LANES), F32),
            jax.ShapeDtypeStruct((CHIPS, EDGE_ROWS, LANES), BF16),
        ),
        in_specs=[smem] + [vmem] * 10,
        out_specs=(vmem,) * 4,
        scratch_shapes=[
            pltpu.VMEM((2, 8 + BLOCK, WIDE), F32),
            pltpu.VMEM((2 * BLOCK, LANES), F32),
            pltpu.VMEM((EDGE_ROWS, LANES), F32),
        ],
        compiler_params=pltpu.CompilerParams(vmem_limit_bytes=40 * 1024 * 1024),
        cost_estimate=pl.CostEstimate(
            flops=4 * BLOCK * 4096 * WIDE, bytes_accessed=6_000_000, transcendentals=0
        ),
    )(pos, slabs, *weights, taps, rates, residues, skip)


def back_kernel(
    pos, sent, sub_states, y_in, gate_in, taps, rates, residues, skip,
    out, edges, carried, mixed, head,
):
    block = pos[0] * 4 + pos[1]
    edges[...] = sent[...].astype(F32)
    tap = [[taps[3 * s + m : 3 * s + m + 1, :] for m in range(3)] for s in range(3)]
    rate = rates[...]
    weight = residues[...]
    decay = jnp.exp(-rate)
    long_decay = jnp.exp(-rate * float(STEPS))
    last = [jnp.exp(-rate * float(BLOCK - 1)), jnp.exp(-rate * float(BLOCK - 2))]

    def rows(chip, zh, start, count):
        return edges[chip, EDGE + 10 * zh + start : EDGE + 10 * zh + start + count, :]

    def own(s, pair):
        return tap[s][0] * pair[0:1], tap[s][0] * pair[1:2] + tap[s][1] * pair[0:1]

    def ahead_of(s, pair):
        return tap[s][1] * pair[1:2] + tap[s][2] * pair[0:1], tap[s][2] * pair[1:2]

    def late(chip, zh, tails):
        first, second = own(0, rows(chip, zh, 0, 2)), own(2, rows(chip, zh, 2, 2))
        one, two = ahead_of(0, tails[0:2]), ahead_of(2, tails[2:4])
        return [
            (first[k] + one[k]) * (second[k] + two[k]) - first[k] * second[k] for k in range(2)
        ]

    carry = [jnp.zeros((MODES, LANES), F32) for _ in range(2)]
    for other in range(CHIPS):
        distance = block - 1 - other
        span = jnp.maximum(distance, 0).astype(F32) * float(BLOCK)
        near = jnp.where(distance >= 0, jnp.exp(-rate * span), 0.0)
        far = jnp.exp(-rate * ((distance + CHIPS).astype(F32) * float(BLOCK)))
        states = []
        for zh in range(2):
            state = (
                edges[other, zh * MODES : (zh + 1) * MODES, :]
                + edges[other, (2 + zh) * MODES : (3 + zh) * MODES, :]
            )
            if other > 0 or zh == 1:
                ahead = (other - 1, zh) if other > 0 else (CHIPS - 1, 0)
                added = late(other, zh, rows(*ahead, 4, 4))
                state = state + last[0] * added[0] + last[1] * added[1]
            states.append(state)
        carry[0] = carry[0] + near * states[0]
        carry[1] = carry[1] + near * states[1] + far * states[0]
    decays = [jnp.broadcast_to(decay[m : m + 1], (SUB, LANES)) for m in range(MODES)]
    growth = jnp.exp(rate)
    gain = skip[...]
    ahead = jnp.maximum(block - 1, 0)
    for zh in range(2):
        tails = rows(ahead, zh, 4, 6)
        if zh == 0:
            tails = jnp.where(block == 0, 0.0, tails)
        else:
            tails = jnp.where(block == 0, rows(CHIPS - 1, 0, 4, 6), tails)
        added = late(block, zh, tails)
        state = carry[zh] + growth * (added[0] + growth * added[1])
        for sub in range(SUB):
            start = zh * SUB * MODES + sub * MODES
            carried[start : start + MODES, :] = weight * state
            state = long_decay * state + sub_states[start : start + MODES, :]
        terms = [
            carried[pl.ds(zh * SUB * MODES + m, SUB, stride=MODES), :] for m in range(MODES)
        ]
        for i in range(STEPS):
            at = pl.ds(zh * BLOCK + i, SUB, stride=STEPS)
            terms = [decays[m] * terms[m] for m in range(MODES)]
            sums = terms
            while len(sums) > 1:
                sums = [sums[k] + sums[k + 1] for k in range(0, len(sums), 2)]
            mixed[at, :] = y_in[at, :] + sums[0]
        early = jnp.sum(weight * growth, axis=0, keepdims=True) * added[1]
        start = zh * BLOCK
        mixed[start : start + 1, :] = mixed[start : start + 1, :] + gain * added[0] - early
        mixed[start + 1 : start + 2, :] = mixed[start + 1 : start + 2, :] + gain * added[1]
        head[...] = gate_in[start : start + 16, :]
        for k, row in enumerate(ahead_of(1, tails[4:6])):
            head[k : k + 1, :] = head[k : k + 1, :] + row
        for c in range(2):
            at = slice(start + c * HALF, start + (c + 1) * HALF)
            gate_rows = (gate_in[at, :] * mixed[at, :]).astype(BF16)
            for zl in range(4):
                out[(2 * zh + c) * 4 + zl] = gate_rows
        first_rows = (head[...] * mixed[start : start + 16, :]).astype(BF16)
        for zl in range(4):
            out[2 * zh * 4 + zl, 0:16, :] = first_rows


def back(pos, edges, sub_states, y, gate, taps, rates, residues, skip):
    vmem = pl.BlockSpec(memory_space=pltpu.VMEM)
    smem = pl.BlockSpec(memory_space=pltpu.SMEM)
    return pl.pallas_call(
        back_kernel,
        out_shape=jax.ShapeDtypeStruct((16, HALF, LANES), BF16),
        in_specs=[smem] + [vmem] * 8,
        out_specs=vmem,
        scratch_shapes=[
            pltpu.VMEM((CHIPS, EDGE_ROWS, LANES), F32),
            pltpu.VMEM((2 * SUB * MODES, LANES), F32),
            pltpu.VMEM((2 * BLOCK, LANES), F32),
            pltpu.VMEM((16, LANES), F32),
        ],
        compiler_params=pltpu.CompilerParams(vmem_limit_bytes=16 * 1024 * 1024),
        cost_estimate=pl.CostEstimate(
            flops=4_000_000, bytes_accessed=800_000, transcendentals=40_000
        ),
    )(pos, edges, sub_states, y, gate, taps, rates, residues, skip)


def out_kernel(pos, gates, weights, out):
    own_zh, own_yh = pos[2], pos[0] // 2
    total = jnp.zeros((HALF, 1024), F32)
    for depth in range(2):
        for flip in range(2):
            high = own_zh if depth == 0 else 1 - own_zh
            zl = high * 2 + (own_yh if flip == 0 else 1 - own_yh)
            left = [gates[(2 * zh + c) * 4 + zl] for zh in range(2) for c in range(2)]
            right = [
                weights[yl, x, c, flip, depth]
                for yl in range(2)
                for x in range(4)
                for c in range(2)
            ]
            total = total + lax.dot_general(
                jnp.concatenate(left, axis=1),
                jnp.concatenate(right, axis=0),
                (((1,), (1,)), ((), ())),
                preferred_element_type=F32,
            )
    out[...] = total.astype(BF16)


def project_out(pos, gates, weights):
    vmem = pl.BlockSpec(memory_space=pltpu.VMEM)
    smem = pl.BlockSpec(memory_space=pltpu.SMEM)
    return pl.pallas_call(
        out_kernel,
        out_shape=jax.ShapeDtypeStruct((HALF, 1024), BF16),
        in_specs=[smem, vmem, vmem],
        out_specs=vmem,
        compiler_params=pltpu.CompilerParams(vmem_limit_bytes=32 * 1024 * 1024),
        cost_estimate=pl.CostEstimate(
            flops=2 * HALF * 2048 * 1024, bytes_accessed=5_000_000, transcendentals=0
        ),
    )(pos, gates, weights)


def split_kernel(weight, *parts):
    group = lax.axis_index("zh") * 2 + lax.axis_index("c")
    for flip, part in enumerate(parts):
        lane = pl.multiple_of((group ^ flip) * LANES, LANES)
        for s in range(3):
            part[:, s * LANES : (s + 1) * LANES] = weight[s, :, pl.ds(lane, LANES)]


def split(in_weight):
    vmem = pl.BlockSpec(memory_space=pltpu.VMEM)
    return pl.pallas_call(
        split_kernel,
        out_shape=(jax.ShapeDtypeStruct((GROUP, WIDE), BF16),) * 4,
        in_specs=[vmem],
        out_specs=(vmem,) * 4,
        compiler_params=pltpu.CompilerParams(vmem_limit_bytes=8 * 1024 * 1024),
    )(in_weight)


def transposed_routes():
    routes = [[], []]
    for zh, yh, yl, x, c, zl in np.ndindex(*SIZES):
        source = int(np.ravel_multi_index((zh, yh, yl, x, c, zl), SIZES))
        for flip in range(2):
            target = ((zl // 2) ^ flip, zl % 2, yl, x, c, zh * 2 + yh)
            routes[flip].append((source, int(np.ravel_multi_index(target, SIZES))))
    return routes


def shards(tokens, in_weight, short_weight, residues, decay_rates, skip_gain, out_weight):
    zh, x, c = (lax.axis_index(axis) for axis in ("zh", "x", "c"))
    y = lax.axis_index(("yh", "yl"))
    pos = jnp.stack([y, x, zh, c]).astype(jnp.int32)
    group = zh * 2 + c

    slabs = lax.all_gather(tokens, ("zh", "zl", "c"), axis=0, tiled=False)
    slabs = slabs.reshape(2, 4, 2, HALF, 1024)

    quarters = split(in_weight)

    def quarter(flip):
        if flip == 0:
            return quarters[0]
        return lax.ppermute(quarters[flip], ("zh", "c"), [(i, i ^ flip) for i in range(4)])

    def in_order(own, other):
        first = jnp.where(c == 0, own, other)
        second = jnp.where(c == 0, other, own)
        return jnp.concatenate([first, second], axis=0)

    far = in_order(quarter(2), quarter(3))
    near = in_order(quarter(0), quarter(1))
    gathered_once = jnp.concatenate(direct(jnp.concatenate([near, far], axis=0), 0), axis=0)

    def own_channels(table, axis):
        return lax.dynamic_slice_in_dim(table, group * LANES, LANES, axis)

    taps = own_channels(short_weight, 2).reshape(9, LANES)
    rates = own_channels(decay_rates, 0).T
    weights = own_channels(residues, 0).T
    skip = own_channels(skip_gain, 0)[None]

    half = gathered_once.shape[0] // 2
    low = crossed(gathered_once, 1, 1)
    high = crossed(gathered_once, 1, -1)
    moved = [lax.ppermute(out_weight.T, AXES, route) for route in transposed_routes()]
    tables = (pos, taps, rates, weights, skip)
    low, high, moved, tables = lax.optimization_barrier((low, high, moved, tables))
    pos, taps, rates, weights, skip = tables
    moved = jnp.concatenate(moved, axis=0)
    far_low = crossed(low[:half], 1, 1)
    far_high = crossed(high[half:], 1, -1)
    flipped = lax.ppermute(moved, "yh", [(0, 1), (1, 0)])
    far_low, far_high, slabs = lax.optimization_barrier((far_low, far_high, slabs))
    far_low, far_high, flipped = lax.optimization_barrier((far_low, far_high, flipped))
    in_weights = [gathered_once, low, high, far_low, far_high]

    slabs, in_weights[3] = lax.optimization_barrier((slabs, in_weights[3]))

    gathered = lax.all_gather(jnp.stack([moved, flipped]), ("yl", "x", "c"), axis=0, tiled=False)
    gathered = gathered.reshape(2, 4, 2, 2, 2, GROUP, 512)

    mixed, gate, sub_states, edges = front(pos, slabs, in_weights, taps, rates, weights, skip)
    edges = lax.all_to_all(edges, PLANE, split_axis=0, concat_axis=0, tiled=True)
    gate_out = back(pos, edges, sub_states, mixed, gate, taps, rates, weights, skip)
    gates = lax.all_to_all(gate_out, ("zh", "c", "zl"), split_axis=0, concat_axis=0, tiled=True)
    return project_out(pos, gates, gathered)


def solution(mesh):
    split_mesh = Mesh(mesh.devices.reshape(SIZES), AXES)
    return jax.shard_map(
        shards,
        mesh=split_mesh,
        in_specs=(
            P(SEQ, "zl"),
            P(None, SEQ, "zl"),
            P(None, None, "zl"),
            P("zl", None),
            P("zl", None),
            P("zl"),
            P("zl", SEQ),
        ),
        out_specs=P(SEQ, "zl"),
        check_vma=False,
    )
```

```python
import functools

import jax
import jax.numpy as jnp
import numpy as np
from jax import lax
from jax.experimental import pallas as pl
from jax.experimental.pallas import tpu as pltpu
from jax.sharding import Mesh, PartitionSpec as P

AXES = ("zh", "yh", "yl", "x", "c", "zl")
SIZES = (2, 2, 2, 4, 2, 4)
SEQ = AXES[:5]
PLANE = ("yh", "yl", "x")
CHIPS = 16
BLOCK = 256
HALF = 128
LANES = 128
WIDE = 3 * LANES
MODES = 8
SUB = 8
STEPS = BLOCK // SUB
EDGE = 4 * MODES
EDGE_ROWS = 56
GROUP = 64
F32 = jnp.float32
BF16 = jnp.bfloat16


def crossed(block, phase, distance):
    route = []
    for y, x, c in np.ndindex(4, 4, 2):
        target = (y, (x + distance) % 4, c) if c != phase else ((y + distance) % 4, x, c)
        route.append((int(np.ravel_multi_index((y, x, c), (4, 4, 2))), int(np.ravel_multi_index(target, (4, 4, 2)))))
    return lax.ppermute(block, PLANE + ("c",), route)


def direct(block, phase):
    return [block] + [crossed(block, phase, distance) for distance in (1, -1, 2)]


RING_ORDER = (0, -1, 1, 2)


def front_kernel(
    pos,
    slabs,
    w0, w1, w2, w3, w4,
    taps,
    rates,
    residues,
    skip,
    y_out,
    gate_out,
    sub_out,
    edge_out,
    proj,
    gated,
    edge,
):
    own_y, own_x, own_zh, own_c = pos[0], pos[1], pos[2], pos[3]

    def features(outer, inner, half):
        first = RING_ORDER[outer] + 4
        second = RING_ORDER[inner] + 4
        at_y = lax.rem(own_y + jnp.where(own_c == 1, first, second), 4)
        at_x = lax.rem(own_x + jnp.where(own_c == 1, second, first), 4)
        at_zh = own_zh if half == 0 else 1 - own_zh
        zl = at_zh * 2 + at_y // 2
        lane = pl.multiple_of((lax.rem(at_y, 2) * 4 + at_x) * 128, 128)
        return slabs[:, pl.ds(zl, 1), :, :, pl.ds(lane, 128)].reshape(2 * BLOCK, 128)

    total = None
    place = 0
    for array in (w0, w1, w2, w3, w4):
        count = array.shape[0] // 256
        parts = [
            features((place + k) // 4, (place + k) % 4, half)
            for k in range(count)
            for half in range(2)
        ]
        part = jnp.dot(jnp.concatenate(parts, axis=1), array[...], preferred_element_type=F32)
        total = part if total is None else total + part
        place += count
    proj[:, 0:8, :] = jnp.zeros((2, 8, WIDE), F32)
    proj[:, 8:, :] = total.astype(BF16).astype(F32).reshape(2, BLOCK, WIDE)
    gain = skip[...]
    for zh in range(2):
        streams = []
        for s in range(3):
            lanes = slice(s * LANES, (s + 1) * LANES)
            tap = [taps[3 * s + m : 3 * s + m + 1, :] for m in range(3)]
            total = jnp.zeros((BLOCK, LANES), F32)
            for m in range(3):
                total = total + tap[m] * proj[zh, 8 - m : 8 - m + BLOCK, lanes]
            streams.append(total)
        gated[zh * BLOCK : (zh + 1) * BLOCK, :] = streams[0] * streams[2]
        gate_out[zh * BLOCK : (zh + 1) * BLOCK, :] = streams[1]
        for k, (s, row) in enumerate(((0, 8), (2, 8), (0, -2), (2, -2), (1, -2))):
            row = row if row > 0 else 8 + BLOCK + row
            start = EDGE + 10 * zh + 2 * k
            edge[start : start + 2, :] = proj[zh, row : row + 2, s * LANES : (s + 1) * LANES]
    edge[EDGE + 20 :, :] = jnp.zeros((EDGE_ROWS - EDGE - 20, LANES), F32)
    rate = rates[...]
    decay = jnp.exp(-rate)
    weight = residues[...]
    decays = [jnp.broadcast_to(decay[m : m + 1], (SUB, LANES)) for m in range(MODES)]
    weights = [jnp.broadcast_to(weight[m : m + 1], (SUB, LANES)) for m in range(MODES)]
    gain = jnp.broadcast_to(gain, (SUB, LANES))
    long_decay = jnp.exp(-rate * float(STEPS))
    for zh in range(2):
        state = [jnp.zeros((SUB, LANES), F32) for _ in range(MODES)]
        for i in range(STEPS):
            rows = pl.ds(zh * BLOCK + i, SUB, stride=STEPS)
            entry = gated[rows, :]
            state = [decays[m] * state[m] + entry for m in range(MODES)]
            terms = [weights[m] * state[m] for m in range(MODES)]
            while len(terms) > 1:
                terms = [terms[k] + terms[k + 1] for k in range(0, len(terms), 2)]
            y_out[rows, :] = terms[0] + gain * entry
        for m in range(MODES):
            sub_out[pl.ds(zh * SUB * MODES + m, SUB, stride=MODES), :] = state[m]
        total = jnp.zeros((MODES, LANES), F32)
        for sub in range(SUB):
            start = zh * SUB * MODES + sub * MODES
            total = long_decay * total + sub_out[start : start + MODES, :]
        upper = total.astype(BF16).astype(F32)
        edge[zh * MODES : (zh + 1) * MODES, :] = upper
        edge[(2 + zh) * MODES : (3 + zh) * MODES, :] = total - upper
    sent = edge[...].astype(BF16)
    for chip in range(CHIPS):
        edge_out[chip] = sent


def front(pos, slabs, weights, taps, rates, residues, skip):
    vmem = pl.BlockSpec(memory_space=pltpu.VMEM)
    smem = pl.BlockSpec(memory_space=pltpu.SMEM)
    return pl.pallas_call(
        front_kernel,
        out_shape=(
            jax.ShapeDtypeStruct((2 * BLOCK, LANES), F32),
            jax.ShapeDtypeStruct((2 * BLOCK, LANES), F32),
            jax.ShapeDtypeStruct((2 * SUB * MODES, LANES), F32),
            jax.ShapeDtypeStruct((CHIPS, EDGE_ROWS, LANES), BF16),
        ),
        in_specs=[smem] + [vmem] * 10,
        out_specs=(vmem,) * 4,
        scratch_shapes=[
            pltpu.VMEM((2, 8 + BLOCK, WIDE), F32),
            pltpu.VMEM((2 * BLOCK, LANES), F32),
            pltpu.VMEM((EDGE_ROWS, LANES), F32),
        ],
        compiler_params=pltpu.CompilerParams(vmem_limit_bytes=40 * 1024 * 1024),
        cost_estimate=pl.CostEstimate(
            flops=4 * BLOCK * 4096 * WIDE, bytes_accessed=6_000_000, transcendentals=0
        ),
    )(pos, slabs, *weights, taps, rates, residues, skip)


def back_kernel(
    pos, sent, sub_states, y_in, gate_in, taps, rates, residues, skip,
    out, edges, carried, mixed, head,
):
    block = pos[0] * 4 + pos[1]
    edges[...] = sent[...].astype(F32)
    tap = [[taps[3 * s + m : 3 * s + m + 1, :] for m in range(3)] for s in range(3)]
    rate = rates[...]
    weight = residues[...]
    decay = jnp.exp(-rate)
    long_decay = jnp.exp(-rate * float(STEPS))
    last = [jnp.exp(-rate * float(BLOCK - 1)), jnp.exp(-rate * float(BLOCK - 2))]

    def rows(chip, zh, start, count):
        return edges[chip, EDGE + 10 * zh + start : EDGE + 10 * zh + start + count, :]

    def own(s, pair):
        return tap[s][0] * pair[0:1], tap[s][0] * pair[1:2] + tap[s][1] * pair[0:1]

    def ahead_of(s, pair):
        return tap[s][1] * pair[1:2] + tap[s][2] * pair[0:1], tap[s][2] * pair[1:2]

    def late(chip, zh, tails):
        first, second = own(0, rows(chip, zh, 0, 2)), own(2, rows(chip, zh, 2, 2))
        one, two = ahead_of(0, tails[0:2]), ahead_of(2, tails[2:4])
        return [
            (first[k] + one[k]) * (second[k] + two[k]) - first[k] * second[k] for k in range(2)
        ]

    carry = [jnp.zeros((MODES, LANES), F32) for _ in range(2)]
    for other in range(CHIPS):
        distance = block - 1 - other
        span = jnp.maximum(distance, 0).astype(F32) * float(BLOCK)
        near = jnp.where(distance >= 0, jnp.exp(-rate * span), 0.0)
        far = jnp.exp(-rate * ((distance + CHIPS).astype(F32) * float(BLOCK)))
        states = []
        for zh in range(2):
            state = (
                edges[other, zh * MODES : (zh + 1) * MODES, :]
                + edges[other, (2 + zh) * MODES : (3 + zh) * MODES, :]
            )
            if other > 0 or zh == 1:
                ahead = (other - 1, zh) if other > 0 else (CHIPS - 1, 0)
                added = late(other, zh, rows(*ahead, 4, 4))
                state = state + last[0] * added[0] + last[1] * added[1]
            states.append(state)
        carry[0] = carry[0] + near * states[0]
        carry[1] = carry[1] + near * states[1] + far * states[0]
    decays = [jnp.broadcast_to(decay[m : m + 1], (SUB, LANES)) for m in range(MODES)]
    growth = jnp.exp(rate)
    gain = skip[...]
    ahead = jnp.maximum(block - 1, 0)
    for zh in range(2):
        tails = rows(ahead, zh, 4, 6)
        if zh == 0:
            tails = jnp.where(block == 0, 0.0, tails)
        else:
            tails = jnp.where(block == 0, rows(CHIPS - 1, 0, 4, 6), tails)
        added = late(block, zh, tails)
        state = carry[zh] + growth * (added[0] + growth * added[1])
        for sub in range(SUB):
            start = zh * SUB * MODES + sub * MODES
            carried[start : start + MODES, :] = weight * state
            state = long_decay * state + sub_states[start : start + MODES, :]
        terms = [
            carried[pl.ds(zh * SUB * MODES + m, SUB, stride=MODES), :] for m in range(MODES)
        ]
        for i in range(STEPS):
            at = pl.ds(zh * BLOCK + i, SUB, stride=STEPS)
            terms = [decays[m] * terms[m] for m in range(MODES)]
            sums = terms
            while len(sums) > 1:
                sums = [sums[k] + sums[k + 1] for k in range(0, len(sums), 2)]
            mixed[at, :] = y_in[at, :] + sums[0]
        early = jnp.sum(weight * growth, axis=0, keepdims=True) * added[1]
        start = zh * BLOCK
        mixed[start : start + 1, :] = mixed[start : start + 1, :] + gain * added[0] - early
        mixed[start + 1 : start + 2, :] = mixed[start + 1 : start + 2, :] + gain * added[1]
        head[...] = gate_in[start : start + 16, :]
        for k, row in enumerate(ahead_of(1, tails[4:6])):
            head[k : k + 1, :] = head[k : k + 1, :] + row
        for c in range(2):
            at = slice(start + c * HALF, start + (c + 1) * HALF)
            gate_rows = (gate_in[at, :] * mixed[at, :]).astype(BF16)
            for zl in range(4):
                out[(2 * zh + c) * 4 + zl] = gate_rows
        first_rows = (head[...] * mixed[start : start + 16, :]).astype(BF16)
        for zl in range(4):
            out[2 * zh * 4 + zl, 0:16, :] = first_rows


def back(pos, edges, sub_states, y, gate, taps, rates, residues, skip):
    vmem = pl.BlockSpec(memory_space=pltpu.VMEM)
    smem = pl.BlockSpec(memory_space=pltpu.SMEM)
    return pl.pallas_call(
        back_kernel,
        out_shape=jax.ShapeDtypeStruct((16, HALF, LANES), BF16),
        in_specs=[smem] + [vmem] * 8,
        out_specs=vmem,
        scratch_shapes=[
            pltpu.VMEM((CHIPS, EDGE_ROWS, LANES), F32),
            pltpu.VMEM((2 * SUB * MODES, LANES), F32),
            pltpu.VMEM((2 * BLOCK, LANES), F32),
            pltpu.VMEM((16, LANES), F32),
        ],
        compiler_params=pltpu.CompilerParams(vmem_limit_bytes=16 * 1024 * 1024),
        cost_estimate=pl.CostEstimate(
            flops=4_000_000, bytes_accessed=800_000, transcendentals=40_000
        ),
    )(pos, edges, sub_states, y, gate, taps, rates, residues, skip)


def out_kernel(pos, gates, weights, out):
    own_zh, own_yh = pos[2], pos[0] // 2
    total = jnp.zeros((HALF, 1024), F32)
    for depth in range(2):
        for flip in range(2):
            high = own_zh if depth == 0 else 1 - own_zh
            zl = high * 2 + (own_yh if flip == 0 else 1 - own_yh)
            left = [gates[(2 * zh + c) * 4 + zl] for zh in range(2) for c in range(2)]
            right = [
                weights[yl, x, c, flip, depth ^ c]
                for yl in range(2)
                for x in range(4)
                for c in range(2)
            ]
            total = total + lax.dot_general(
                jnp.concatenate(left, axis=1),
                jnp.concatenate(right, axis=0),
                (((1,), (1,)), ((), ())),
                preferred_element_type=F32,
            )
    out[...] = total.astype(BF16)


def project_out(pos, gates, weights):
    vmem = pl.BlockSpec(memory_space=pltpu.VMEM)
    smem = pl.BlockSpec(memory_space=pltpu.SMEM)
    return pl.pallas_call(
        out_kernel,
        out_shape=jax.ShapeDtypeStruct((HALF, 1024), BF16),
        in_specs=[smem, vmem, vmem],
        out_specs=vmem,
        compiler_params=pltpu.CompilerParams(vmem_limit_bytes=32 * 1024 * 1024),
        cost_estimate=pl.CostEstimate(
            flops=2 * HALF * 2048 * 1024, bytes_accessed=5_000_000, transcendentals=0
        ),
    )(pos, gates, weights)


def split_kernel(weight, *parts):
    group = lax.axis_index("zh") * 2 + lax.axis_index("c")
    for flip, part in enumerate(parts):
        lane = pl.multiple_of((group ^ flip) * LANES, LANES)
        for s in range(3):
            part[:, s * LANES : (s + 1) * LANES] = weight[s, :, pl.ds(lane, LANES)]


def split(in_weight):
    vmem = pl.BlockSpec(memory_space=pltpu.VMEM)
    return pl.pallas_call(
        split_kernel,
        out_shape=(jax.ShapeDtypeStruct((GROUP, WIDE), BF16),) * 4,
        in_specs=[vmem],
        out_specs=(vmem,) * 4,
        compiler_params=pltpu.CompilerParams(vmem_limit_bytes=8 * 1024 * 1024),
    )(in_weight)


def transposed_routes():
    routes = [[], []]
    for zh, yh, yl, x, c, zl in np.ndindex(*SIZES):
        source = int(np.ravel_multi_index((zh, yh, yl, x, c, zl), SIZES))
        for flip in range(2):
            target = ((zl // 2) ^ flip ^ c, zl % 2, yl, x, c, zh * 2 + yh)
            routes[flip].append((source, int(np.ravel_multi_index(target, SIZES))))
    return routes


def shards(tokens, in_weight, short_weight, residues, decay_rates, skip_gain, out_weight):
    zh, x, c = (lax.axis_index(axis) for axis in ("zh", "x", "c"))
    y = lax.axis_index(("yh", "yl"))
    pos = jnp.stack([y, x, zh, c]).astype(jnp.int32)
    group = zh * 2 + c

    slabs = lax.all_gather(tokens, ("zh", "zl", "c"), axis=0, tiled=False)
    slabs = slabs.reshape(2, 4, 2, HALF, 1024)

    quarters = split(in_weight)

    def quarter(flip):
        if flip == 0:
            return quarters[0]
        return lax.ppermute(quarters[flip], ("zh", "c"), [(i, i ^ flip) for i in range(4)])

    def in_order(own, other):
        first = jnp.where(c == 0, own, other)
        second = jnp.where(c == 0, other, own)
        return jnp.concatenate([first, second], axis=0)

    far = in_order(quarter(2), quarter(3))
    near = in_order(quarter(0), quarter(1))
    gathered_once = jnp.concatenate(direct(jnp.concatenate([near, far], axis=0), 0), axis=0)

    def own_channels(table, axis):
        return lax.dynamic_slice_in_dim(table, group * LANES, LANES, axis)

    taps = own_channels(short_weight, 2).reshape(9, LANES)
    rates = own_channels(decay_rates, 0).T
    weights = own_channels(residues, 0).T
    skip = own_channels(skip_gain, 0)[None]

    half = gathered_once.shape[0] // 2
    low = crossed(gathered_once, 1, 1)
    high = crossed(gathered_once, 1, -1)
    moved = [lax.ppermute(out_weight.T, AXES, route) for route in transposed_routes()]
    tables = (pos, taps, rates, weights, skip)
    low, high, moved, tables = lax.optimization_barrier((low, high, moved, tables))
    pos, taps, rates, weights, skip = tables
    moved = jnp.concatenate(moved, axis=0)
    far_low = crossed(low[:half], 1, 1)
    far_high = crossed(high[half:], 1, -1)
    flipped = lax.ppermute(moved, "yh", [(0, 1), (1, 0)])
    far_low, far_high, slabs = lax.optimization_barrier((far_low, far_high, slabs))
    far_low, far_high, flipped = lax.optimization_barrier((far_low, far_high, flipped))
    in_weights = [gathered_once, low, high, far_low, far_high]

    slabs, in_weights[3] = lax.optimization_barrier((slabs, in_weights[3]))

    gathered = lax.all_gather(jnp.stack([moved, flipped]), ("yl", "x", "c"), axis=0, tiled=False)
    gathered = gathered.reshape(2, 4, 2, 2, 2, GROUP, 512)

    mixed, gate, sub_states, edges = front(pos, slabs, in_weights, taps, rates, weights, skip)
    edges = lax.all_to_all(edges, PLANE, split_axis=0, concat_axis=0, tiled=True)
    gate_out = back(pos, edges, sub_states, mixed, gate, taps, rates, weights, skip)
    gates = lax.all_to_all(gate_out, ("zh", "c", "zl"), split_axis=0, concat_axis=0, tiled=True)
    return project_out(pos, gates, gathered)


def solution(mesh):
    split_mesh = Mesh(mesh.devices.reshape(SIZES), AXES)
    return jax.shard_map(
        shards,
        mesh=split_mesh,
        in_specs=(
            P(SEQ, "zl"),
            P(None, SEQ, "zl"),
            P(None, None, "zl"),
            P("zl", None),
            P("zl", None),
            P("zl"),
            P("zl", SEQ),
        ),
        out_specs=P(SEQ, "zl"),
        check_vma=False,
    )
```
